32 devices in a mesh: groups: 2 (over y), center: 8 (over z, x), row: 2 (over core).
Axes of the slice: x: 2, y: 2, z: 4, core: 2. Of those that a mesh axis runs over, the one named last changes fastest.
Arguments:
- dataset: float32 [512, 1024], P(('groups', 'center', 'row')), parts along dimension 0, may hold values from -0.1875 to 0.1875
- centers: float32 [2048, 1024], P(('groups', 'center')), parts along dimension 0, may hold values from -0.1875 to 0.1875
- weights: float32 [2048, 512], P(('groups', 'center'), 'row'), parts along dimension 0, may hold values from -0.1875 to 0.1875
- batch_index: int32 [2, 128], P(None, ('groups', 'center', 'row')), parts along dimension 1, may hold values from 0 to 15
- targets: float32 [2, 128, 512], P(None, ('groups', 'center', 'row')), parts along dimension 1, may hold values from -6 to 6
- gamma: float32 [2], P('groups'), parts along dimension 0, may hold values from 0.3 to 1.5
Outputs:
- new_weights: float32 [2048, 512], P(('groups', 'center'), 'row'), parts along dimension 0
- residual: float32 [128, 512], P(('groups', 'center', 'row')), parts along dimension 0
The draws below stay inside these ranges and needn't reach their ends.
There are 2 independent parts, one for each index of `groups`. The reference program is written for one: setup_inputs(seed, part) draws one part's arguments, and reference() takes and returns one part's arrays. A program takes and returns all parts, laid end to end along the dimension named above; each array names one. Nothing has to cross between parts.
Inputs may be any that keep to these rules, and one draw needn't show every extreme that they name: `batch_index`: each entry picks a row within the block of 16 dataset rows that has the same block number as the entry's block of 4 batch rows.
All inputs are finite; a program needn't handle non-finite values.
Results may differ from the reference program's by a relative error of at most 0.0001.
Values sent between devices are 32-bit elements; how exact they have to be, the bound alone decides.
A program may use at most 64 MiB of HBM per device.

```python
import math
import jax
import jax.numpy as jnp
from jax import lax

F = 1024
K = 512
ROWS_DEV = 4
DATA_DEV = 16
CENTERS = 1024
BATCH = 64
NDATA = 256
N_CENTER = 8
N_ROW = 2


def shared_centroids(key):
    centroid = jax.random.normal(jax.random.fold_in(key, 5), (64, F), jnp.float32) * F ** (-0.5)
    return centroid


def clustered(key, amount, seed_tag):
    centroid = shared_centroids(key)
    member = jax.random.randint(jax.random.fold_in(key, seed_tag), (amount,), 0, 64)
    chosen = centroid[member]
    jitter = jax.random.normal(jax.random.fold_in(key, seed_tag + 1), (amount, F), jnp.float32)
    points = chosen + jitter * (0.5 * F ** (-0.5))
    return jnp.clip(points, -6.0 * F ** (-0.5), 6.0 * F ** (-0.5))


def draw_dataset(key, part):
    return clustered(key, NDATA, 21)


def draw_centers(key, part):
    return clustered(key, CENTERS, 31)


def touch_ends(entries, own_key, least, top_value):
    longest = entries.shape.index(max(entries.shape))
    spots = []
    for shift in (0, 1):
        where = [jax.random.randint(jax.random.fold_in(own_key, axis), (), 0, length) for axis, length in enumerate(entries.shape)]
        where[longest] = (where[longest] + shift) % entries.shape[longest]
        spots.append(tuple(where))
    return entries.at[spots[0]].set(least).at[spots[1]].set(top_value)


def steps_of(stream_key, extent, split, least, top_value):
    def one(position, blocks):
        heights = jax.random.uniform(jax.random.fold_in(jax.random.fold_in(stream_key, 6), position), (blocks,), jnp.float32, least / len(split), top_value / len(split))
        return jnp.repeat(jnp.exp(heights), extent[position] // blocks).reshape((-1,) + (1,) * (len(extent) - position - 1))

    factor_of = one(*split[0])
    for cut in split[1:]:
        factor_of = factor_of * one(*cut)
    return factor_of


def noise(own_key, extent, width, most, shards=(), held_as=jnp.bfloat16):
    result = width * jax.random.normal(own_key, extent, jnp.float32)
    if shards:
        result = result * steps_of(own_key, extent, shards, -0.22, 0.18)
    return jnp.clip(result, -most, most).astype(held_as)


def setup_inputs(seed: int = 0, part: int = 0) -> dict:
    key_of = jax.random.split(jax.random.key(seed), 7)
    part_keys = jax.random.split(jax.random.fold_in(key_of[6], part), 7)
    return {
        "dataset": draw_dataset(jax.random.fold_in(jax.random.fold_in(key_of[6], part), 71), part),
        "centers": draw_centers(jax.random.fold_in(jax.random.fold_in(key_of[6], part), 71), part),
        "weights": noise(part_keys[2], (CENTERS, K), CENTERS ** -0.5, 0.1875, ((0, 8), (1, 2)), jnp.float32),
        "batch_index": touch_ends(jax.random.randint(part_keys[3], (2, BATCH), 0, DATA_DEV), jax.random.fold_in(part_keys[3], 1), 0, DATA_DEV - 1).astype(jnp.int32),
        "targets": noise(part_keys[4], (2, BATCH, K), 1.0, 6.0, ((1, 16),), jnp.float32),
        "gamma": jnp.clip(jnp.exp(jax.random.uniform(part_keys[5], (1,), jnp.float32, math.log(0.3), math.log(1.5))), 0.3, 1.5),
    }


def reference(dataset, centers, weights, batch_index, targets, gamma):
    blocks = N_CENTER * N_ROW
    grouped = dataset.reshape(blocks, DATA_DEV, F)
    center_sq = jnp.sum(centers * centers, axis=1)
    current = weights
    residual = None
    for step in range(2):
        picks = batch_index[step].reshape(blocks, ROWS_DEV)
        rows = jnp.take_along_axis(grouped, picks[:, :, None], axis=1).reshape(BATCH, F)
        row_sq = jnp.sum(rows * rows, axis=1)
        cross = jnp.dot(rows, centers.T, precision=lax.Precision.HIGHEST, preferred_element_type=jnp.float32)
        kernel = jnp.exp(-gamma[0] * (row_sq[:, None] + center_sq[None, :] - 2.0 * cross))
        predict = jnp.dot(kernel, current, precision=lax.Precision.HIGHEST, preferred_element_type=jnp.float32)
        residual = predict - targets[step]
        grad = jnp.dot(kernel.T, residual, precision=lax.Precision.HIGHEST, preferred_element_type=jnp.float32)
        current = current - (0.5 / BATCH) * grad
    return current, residual
```

```python
import functools

import jax
import jax.numpy as jnp
from jax import lax
from jax.experimental import pallas as pl
from jax.experimental.pallas import tpu as pltpu
from jax.sharding import PartitionSpec as P

MESH = pl.DeviceIdType.MESH
LANES = 128
NN = (((1,), (0,)), ((), ()))
NT = (((1,), (1,)), ((), ()))
UNROLL = 8


def split(v):
    hi = v.astype(jnp.bfloat16)
    return hi, (v - hi.astype(jnp.float32)).astype(jnp.bfloat16)


def dot3(a, b, dims=NN):
    (ah, al), (bh, bl) = a, b
    dot = functools.partial(lax.dot_general, dimension_numbers=dims, preferred_element_type=jnp.float32)
    return dot(ah, bh) + (dot(ah, bl) + dot(al, bh))


def each(lo, hi, body):
    if hi - lo <= UNROLL:
        for d in range(lo, hi):
            body(d)
    else:
        lax.fori_loop(lo, hi, lambda d, _: (body(d), 0)[1], 0)


def kernel(
    n, ds_ref, cen_ref, w_ref, idx_ref, tgt_ref, gam_ref, w_out, res_out,
    xbuf, kbuf, tsib, tplace, part, rs_in, allv, res_s, rsend, rrecv,
    x_ss, x_rs, p_ss, p_rs, a_ss, a_rs, s_ss, s_rs,
):
    f32 = jnp.float32
    c, r = lax.axis_index("center"), lax.axis_index("row")
    sib = 1 - r
    steps, rows = idx_ref.shape
    slot = steps * rows
    chunks = 2 * n
    total = slot * chunks
    batch = rows * chunks
    cols = w_ref.shape[1]
    ncen = cen_ref.shape[0]
    rate = 0.5 / batch
    rp, rg = total // n, batch // n
    pw, gw = cols // LANES, pl.cdiv(batch, LANES)

    barrier = pltpu.get_barrier_semaphore()

    def greet(d):
        pl.semaphore_signal(
            barrier, inc=1, device_id={"center": lax.rem(c + d, n), "row": r}, device_id_type=MESH
        )

    each(1, n, greet)
    pl.semaphore_signal(barrier, inc=1, device_id={"center": c, "row": sib}, device_id_type=MESH)

    def copy(src, dst, ss, rs, peer):
        return pltpu.make_async_remote_copy(
            src_ref=src, dst_ref=dst, send_sem=ss, recv_sem=rs, device_id=peer, device_id_type=MESH
        )

    def to(d):
        return {"center": lax.rem(c + d, n), "row": r}

    to_sib = {"center": c, "row": sib}

    for b in range(steps):
        for i in range(rows):
            xbuf[c, pl.ds(b * rows + i, 1), :] = ds_ref[pl.ds(idx_ref[b, i], 1), :]

    pl.semaphore_wait(barrier, n)

    def x_copy(d):
        return copy(xbuf.at[c], xbuf.at[c], x_ss.at[d], x_rs.at[d], to(d))

    each(1, n, lambda d: x_copy(d).start())
    sib_cols = pl.ds(pl.multiple_of(sib * cols, LANES), cols)
    own_cols = pl.ds(pl.multiple_of(r * cols, LANES), cols)
    t_copy = copy(tgt_ref.at[:, :, sib_cols], tsib, s_ss.at[0], s_rs.at[0], to_sib)
    t_copy.start()

    cen = cen_ref[...]
    cen2 = split(cen)
    csq = jnp.sum(cen * cen, axis=1, keepdims=True)
    csq = jnp.transpose(jnp.broadcast_to(csq, (ncen, ncen)))[0:1, :]
    w2 = split(w_ref[...])
    gamma = gam_ref[0]

    t_copy.wait()
    chunk_id = lax.broadcasted_iota(jnp.int32, (chunks, cols), 0)
    for b in range(steps):
        mine, other = tgt_ref[b, :, own_cols], tsib[b]
        for i in range(rows):
            j = b * rows + i
            placed = jnp.where(chunk_id == r * n + c, mine[i : i + 1, :], 0.0)
            placed = jnp.where(chunk_id == sib * n + c, other[i : i + 1, :], placed)
            tplace[pl.ds(j * chunks, chunks), :] = placed

    each(1, n, lambda d: x_copy(d).wait_recv())

    blocks = max(1, n // UNROLL)
    per = n // blocks
    k_base = pl.multiple_of(r * (n * slot), slot)

    def kernel_rows(s):
        x = xbuf[pl.ds(s * per, per)].reshape(per * slot, xbuf.shape[2])
        xsq = jnp.sum(x * x, axis=1, keepdims=True)
        cross = dot3(split(x), cen2, NT)
        kbuf[pl.ds(pl.multiple_of(k_base + s * (per * slot), slot), per * slot), :] = jnp.exp(
            -gamma * (xsq + csq - 2.0 * cross)
        )

    each(0, blocks, kernel_rows)
    k_rows = pl.ds(k_base, n * slot)
    k_copy = copy(kbuf.at[k_rows, :], kbuf.at[k_rows, :], s_ss.at[1], s_rs.at[1], to_sib)
    k_copy.start()
    k_copy.wait()

    k_all = jnp.concatenate([kbuf[pl.ds(j, chunks, stride=slot), :] for j in range(slot)], axis=0)
    kh, kl = split(k_all)
    k0 = (kh[: gw * LANES], kl[: gw * LANES])
    k_t = split(jnp.transpose(k_all))

    for s in range(blocks):
        own = pl.ds(s * per, per)
        lo, hi = s * per * rp, (s + 1) * per * rp
        p = dot3((kh[lo:hi], kl[lo:hi]), w2) - tplace[lo:hi, :]
        lo, hi = batch + s * per * rg, batch + (s + 1) * per * rg
        g = dot3((kh[lo:hi], kl[lo:hi]), k0, NT)
        for l in range(pw):
            part[own, l * rp : (l + 1) * rp, :] = p[:, l * LANES : (l + 1) * LANES].reshape(per, rp, LANES)
        for l in range(gw):
            at = pw * rp + l * rg
            part[own, at : at + rg, :] = g[:, l * LANES : (l + 1) * LANES].reshape(per, rg, LANES)

    def p_copy(d):
        return copy(part.at[lax.rem(c + d, n)], rs_in.at[d], p_ss.at[d], p_rs.at[d], to(d))

    each(1, n, lambda d: p_copy(d).start())
    allv[c] = part[c]

    def add(d):
        p_copy(d).wait_recv()
        allv[c] += rs_in[d]

    each(1, n, add)

    def a_copy(d):
        return copy(allv.at[c], allv.at[c], a_ss.at[d], a_rs.at[d], to(d))

    each(1, n, lambda d: a_copy(d).start())
    each(1, n, lambda d: a_copy(d).wait_recv())

    def whole(at, size, width):
        pieces = [
            allv[:, at + l * size : at + (l + 1) * size, :].reshape(n * size, LANES) for l in range(width)
        ]
        return pieces[0] if width == 1 else jnp.concatenate(pieces, axis=1)

    a = whole(0, rp, pw)
    g = whole(pw * rp, rg, gw)
    res0 = a[:batch]
    pad = gw * LANES - batch
    res0_pad = jnp.concatenate([res0, jnp.zeros((pad, cols), f32)], axis=0) if pad else res0
    res1 = a[batch:] - rate * dot3(split(g), split(res0_pad))
    res_s[...] = res1
    for i in range(rows):
        rsend[i : i + 1, :] = res_s[pl.ds(i * chunks + sib * n + c, 1), :]
    r_copy = copy(rsend, rrecv, s_ss.at[2], s_rs.at[2], to_sib)
    r_copy.start()
    for i in range(rows):
        res_out[i : i + 1, own_cols] = res_s[pl.ds(i * chunks + r * n + c, 1), :]
    res = jnp.concatenate([res0, res1], axis=0)
    w_out[...] = w_ref[...] - rate * dot3(k_t, split(res))
    r_copy.wait()
    res_out[:, sib_cols] = rrecv[...]

    def drain(d):
        x_copy(d).wait_send()
        p_copy(d).wait_send()
        a_copy(d).wait_send()

    each(1, n, drain)


def solution(mesh):
    n = mesh.shape["center"]

    def per_device(dataset, centers, weights, batch_index, targets, gamma):
        f32 = jnp.float32
        steps, rows = batch_index.shape
        slot, feats = steps * rows, dataset.shape[1]
        ncen, cols = weights.shape
        total, batch = slot * 2 * n, rows * 2 * n
        rp, rg = total // n, batch // n
        pw, gw = cols // LANES, pl.cdiv(batch, LANES)
        height = pw * rp + gw * rg
        vm = pltpu.VMEM
        dma = pltpu.SemaphoreType.DMA
        return pl.pallas_call(
            functools.partial(kernel, n),
            out_shape=(
                jax.ShapeDtypeStruct(weights.shape, f32),
                jax.ShapeDtypeStruct(targets.shape[1:], f32),
            ),
            in_specs=[
                pl.BlockSpec(memory_space=pltpu.VMEM),
                pl.BlockSpec(memory_space=pltpu.VMEM),
                pl.BlockSpec(memory_space=pltpu.VMEM),
                pl.BlockSpec(memory_space=pltpu.SMEM),
                pl.BlockSpec(memory_space=pltpu.VMEM),
                pl.BlockSpec(memory_space=pltpu.SMEM),
            ],
            out_specs=(pl.BlockSpec(memory_space=pltpu.VMEM), pl.BlockSpec(memory_space=pltpu.VMEM)),
            scratch_shapes=[
                vm((n, slot, feats), f32),
                vm((2 * n * slot, ncen), f32),
                vm((steps, rows, cols), f32),
                vm((total, cols), f32),
                vm((n, height, LANES), f32),
                vm((n, height, LANES), f32),
                vm((n, height, LANES), f32),
                vm((batch, cols), f32),
                vm((rows, cols), f32),
                vm((rows, cols), f32),
                dma((n,)), dma((n,)), dma((n,)), dma((n,)), dma((n,)), dma((n,)), dma((3,)), dma((3,)),
            ],
            compiler_params=pltpu.CompilerParams(
                collective_id=0, has_side_effects=True, vmem_limit_bytes=56 * 2**20
            ),
        )(dataset, centers, weights, batch_index, targets, gamma)

    return jax.shard_map(
        per_device,
        mesh=mesh,
        in_specs=(
            P(("groups", "center", "row"), None),
            P(("groups", "center"), None),
            P(("groups", "center"), "row"),
            P(None, ("groups", "center", "row")),
            P(None, ("groups", "center", "row"), None),
            P("groups"),
        ),
        out_specs=(P(("groups", "center"), "row"), P(("groups", "center", "row"), None)),
        check_vma=False,
    )
```

```python
import functools

import jax
import jax.numpy as jnp
from jax import lax
from jax.experimental import pallas as pl
from jax.experimental.pallas import tpu as pltpu
from jax.sharding import PartitionSpec as P

MESH = pl.DeviceIdType.MESH
LANES = 128
NN = (((1,), (0,)), ((), ()))
NT = (((1,), (1,)), ((), ()))
UNROLL = 8


def split(v):
    hi = v.astype(jnp.bfloat16)
    return hi, (v - hi.astype(jnp.float32)).astype(jnp.bfloat16)


def dot3(a, b, dims=NN):
    (ah, al), (bh, bl) = a, b
    dot = functools.partial(lax.dot_general, dimension_numbers=dims, preferred_element_type=jnp.float32)
    return dot(ah, bh) + (dot(ah, bl) + dot(al, bh))


def each(lo, hi, body):
    if hi - lo <= UNROLL:
        for d in range(lo, hi):
            body(d)
    else:
        lax.fori_loop(lo, hi, lambda d, _: (body(d), 0)[1], 0)


def kernel(
    n, ds_hbm, cen_hbm, w_hbm, idx_hbm, tgt_hbm, gam_hbm, w_out, res_out,
    ds_ref, cen_ref, w_ref, idx_ref, tgt_ref, gam_ref,
    xbuf, kbuf, tsib, tplace, part, rs_in, allv, res_s, rsend, rrecv,
    in_s, x_ss, x_rs, f_ss, f_rs, p_ss, p_rs, a_ss, a_rs, s_ss, s_rs,
):
    f32 = jnp.float32
    c, r = lax.axis_index("center"), lax.axis_index("row")
    sib = 1 - r
    half = n // 2
    h, side = c // 2, lax.rem(c, 2)
    place = side * half + h
    steps, rows = idx_ref.shape
    slot = steps * rows
    chunks = 2 * n
    batch = rows * chunks
    cols = w_ref.shape[1]
    ncen = cen_ref.shape[0]
    rate = 0.5 / batch
    fold, rp, rg, pw, gw = sizes(n, batch, steps, cols)

    ins = [
        pltpu.make_async_copy(src, dst, in_s.at[i])
        for i, (src, dst) in enumerate(
            [(idx_hbm, idx_ref), (ds_hbm, ds_ref), (tgt_hbm, tgt_ref), (cen_hbm, cen_ref), (w_hbm, w_ref), (gam_hbm, gam_ref)]
        )
    ]
    for one in ins:
        one.start()

    barrier = pltpu.get_barrier_semaphore()

    def to(d):
        return {"center": lax.rem(c + d, n), "row": r}

    to_sib = {"center": c, "row": sib}
    to_pair = {"center": 2 * h + 1 - side, "row": r}
    each(1, n, lambda d: pl.semaphore_signal(barrier, inc=1, device_id=to(d), device_id_type=MESH))
    pl.semaphore_signal(barrier, inc=1, device_id=to_sib, device_id_type=MESH)

    def copy(src, dst, ss, rs, peer):
        return pltpu.make_async_remote_copy(
            src_ref=src, dst_ref=dst, send_sem=ss, recv_sem=rs, device_id=peer, device_id_type=MESH
        )

    ins[0].wait()
    ins[1].wait()
    for b in range(steps):
        for i in range(rows):
            xbuf[place, pl.ds(b * rows + i, 1), :] = ds_ref[pl.ds(idx_ref[b, i], 1), :]
    ins[2].wait()

    pl.semaphore_wait(barrier, n)

    def x_copy(e):
        peer = {"center": 2 * lax.rem(h + e, half) + side, "row": r}
        return copy(xbuf.at[place], xbuf.at[place], x_ss.at[e], x_rs.at[e], peer)

    def f_copy(e):
        at = side * half + lax.rem(h + half - e, half)
        return copy(xbuf.at[at], xbuf.at[at], f_ss.at[e], f_rs.at[e], to_pair)

    each(1, half, lambda e: x_copy(e).start())
    f_copy(0).start()
    sib_cols = pl.ds(pl.multiple_of(sib * cols, LANES), cols)
    own_cols = pl.ds(pl.multiple_of(r * cols, LANES), cols)
    t_copy = copy(tgt_ref.at[:, :, sib_cols], tsib, s_ss.at[0], s_rs.at[0], to_sib)
    t_copy.start()

    ins[3].wait()
    cen = cen_ref[...]
    cen2 = split(cen)
    csq = jnp.sum(cen * cen, axis=1, keepdims=True)
    csq = jnp.transpose(jnp.broadcast_to(csq, (ncen, ncen)))[0:1, :]
    ins[4].wait()
    w2 = split(w_ref[...])
    ins[5].wait()
    gamma = gam_ref[0]

    def pass_on(e):
        x_copy(e).wait_recv()
        f_copy(e).start()

    each(1, half, pass_on)

    count = half * slot
    step = min(count, UNROLL * slot)

    def kernel_rows(which, s):
        first = pl.multiple_of(which * count + s * step, slot)
        x = xbuf[pl.ds(which * half + s * (step // slot), step // slot)].reshape(step, xbuf.shape[2])
        xsq = jnp.sum(x * x, axis=1, keepdims=True)
        cross = dot3(split(x), cen2, NT)
        kbuf[pl.ds(pl.multiple_of(r * (n * slot) + first, slot), step), :] = jnp.exp(
            -gamma * (xsq + csq - 2.0 * cross)
        )

    def k_copy(i, which):
        at = pl.ds(pl.multiple_of(r * (n * slot) + which * count, slot), count)
        return copy(kbuf.at[at, :], kbuf.at[at, :], s_ss.at[i], s_rs.at[i], to_sib)

    each(0, count // step, lambda s: kernel_rows(side, s))
    k_copy(1, side).start()

    t_copy.wait()
    chunk_id = lax.broadcasted_iota(jnp.int32, (chunks, cols), 0)
    for b in range(steps):
        mine, other = tgt_ref[b, :, own_cols], tsib[b]
        for i in range(rows):
            j = b * rows + i
            placed = jnp.where(chunk_id == r * n + place, mine[i : i + 1, :], 0.0)
            placed = jnp.where(chunk_id == sib * n + place, other[i : i + 1, :], placed)
            tplace[pl.ds(j * chunks, chunks), :] = placed

    each(0, half, lambda e: f_copy(e).wait_recv())
    each(0, count // step, lambda s: kernel_rows(1 - side, s))
    k_copy(2, 1 - side).start()
    k_copy(1, side).wait()
    k_copy(2, 1 - side).wait()

    k_all = jnp.concatenate([kbuf[pl.ds(j, chunks, stride=slot), :] for j in range(slot)], axis=0)
    kh, kl = split(k_all)
    k0 = (jnp.concatenate([kh[:batch]] * fold, axis=0), jnp.concatenate([kl[:batch]] * fold, axis=0))

    blocks = max(1, n // UNROLL)
    per = n // blocks
    for s in range(blocks):
        lo, hi = s * per * rp, (s + 1) * per * rp
        p = dot3((kh[lo:hi], kl[lo:hi]), w2) - tplace[lo:hi, :]
        lo, hi = batch + s * per * rg * fold, batch + (s + 1) * per * rg * fold
        g = fold_rows(dot3((kh[lo:hi], kl[lo:hi]), k0, NT), fold, batch)
        for o in range(per):
            for l in range(pw):
                part[s * per + o, l * rp : (l + 1) * rp, :] = p[o * rp : (o + 1) * rp, l * LANES : (l + 1) * LANES]
            for l in range(gw):
                at = pw * rp + l * rg
                part[s * per + o, at : at + rg, :] = g[o * rg : (o + 1) * rg, l * LANES : (l + 1) * LANES]

    def p_copy(d):
        return copy(part.at[lax.rem(c + d, n)], rs_in.at[d], p_ss.at[d], p_rs.at[d], to(d))

    each(1, n, lambda d: p_copy(d).start())
    k_t = split(jnp.transpose(k_all))
    allv[c] = part[c]

    def add(d):
        p_copy(d).wait_recv()
        allv[c] += rs_in[d]

    each(1, n, add)

    def a_copy(d):
        return copy(allv.at[c], allv.at[c], a_ss.at[d], a_rs.at[d], to(d))

    each(1, n, lambda d: a_copy(d).start())
    each(1, n, lambda d: a_copy(d).wait_recv())

    def whole(at, size, width):
        pieces = [
            jnp.concatenate([allv[o, at + l * size : at + (l + 1) * size, :] for o in range(n)], axis=0)
            for l in range(width)
        ]
        return pieces[0] if width == 1 else jnp.concatenate(pieces, axis=1)

    a = whole(0, rp, pw)
    g = unfold_rows(whole(pw * rp, rg, gw), fold, batch)
    res0 = a[:batch]
    res0h, res0l = split(res0)
    res0f = (jnp.concatenate([res0h] * fold, axis=0), jnp.concatenate([res0l] * fold, axis=0))
    res1 = a[batch:] - rate * dot3(split(g), res0f)
    res_s[...] = res1
    for i in range(rows):
        rsend[i : i + 1, :] = res_s[pl.ds(i * chunks + sib * n + place, 1), :]
    r_copy = copy(rsend, rrecv, s_ss.at[3], s_rs.at[3], to_sib)
    r_copy.start()
    for i in range(rows):
        res_out[i : i + 1, own_cols] = res_s[pl.ds(i * chunks + r * n + place, 1), :]
    res1h, res1l = split(res1)
    res = (jnp.concatenate([res0h, res1h], axis=0), jnp.concatenate([res0l, res1l], axis=0))
    w_out[...] = w_ref[...] - rate * dot3(k_t, res)
    r_copy.wait()
    res_out[:, sib_cols] = rrecv[...]

    def drain(d):
        p_copy(d).wait_send()
        a_copy(d).wait_send()

    each(1, n, drain)
    each(1, half, lambda e: x_copy(e).wait_send())
    each(0, half, lambda e: f_copy(e).wait_send())


def sizes(n, batch, steps, cols):
    fold = max(1, LANES // batch)
    return fold, steps * batch // n, batch // fold // n, cols // LANES, pl.cdiv(batch, LANES)


def fold_rows(g, fold, batch):
    if fold == 1:
        return g
    height = g.shape[0] // fold
    at = lax.broadcasted_iota(jnp.int32, (height, LANES), 1) // batch
    out = g[:height]
    for f in range(1, fold):
        out = jnp.where(at == f, g[f * height : (f + 1) * height], out)
    return out


def unfold_rows(g, fold, batch):
    if fold == 1:
        return g
    at = lax.broadcasted_iota(jnp.int32, g.shape, 1) // batch
    return jnp.concatenate([jnp.where(at == f, g, 0.0) for f in range(fold)], axis=0)


def hand_over(w_in, res_in, w_out, res_out, sems):
    copies = [
        pltpu.make_async_copy(w_in, w_out, sems.at[0]),
        pltpu.make_async_copy(res_in, res_out, sems.at[1]),
    ]
    for one in copies:
        one.start()
    for one in copies:
        one.wait()


def solution(mesh):
    n = mesh.shape["center"]

    def per_device(dataset, centers, weights, batch_index, targets, gamma):
        f32 = jnp.float32
        steps, rows = batch_index.shape
        slot, feats = steps * rows, dataset.shape[1]
        ncen, cols = weights.shape
        total, batch = slot * 2 * n, rows * 2 * n
        fold, rp, rg, pw, gw = sizes(n, batch, steps, cols)
        height = pw * rp + gw * rg
        half = n // 2
        vm = pltpu.VMEM
        dma = pltpu.SemaphoreType.DMA
        anywhere = pl.BlockSpec(memory_space=pltpu.HBM)
        outs = (
            jax.ShapeDtypeStruct(weights.shape, f32),
            jax.ShapeDtypeStruct(targets.shape[1:], f32),
        )
        results = pl.pallas_call(
            functools.partial(kernel, n),
            out_shape=outs,
            in_specs=[anywhere] * 6,
            out_specs=(pl.BlockSpec(memory_space=pltpu.VMEM), pl.BlockSpec(memory_space=pltpu.VMEM)),
            scratch_shapes=[
                vm(dataset.shape, f32), vm(centers.shape, f32), vm(weights.shape, f32),
                pltpu.SMEM(batch_index.shape, jnp.int32), vm(targets.shape, f32), pltpu.SMEM(gamma.shape, f32),
                vm((n, slot, feats), f32),
                vm((2 * n * slot, ncen), f32),
                vm((steps, rows, cols), f32),
                vm((total, cols), f32),
                vm((n, height, LANES), f32),
                vm((n, height, LANES), f32),
                vm((n, height, LANES), f32),
                vm((batch, cols), f32),
                vm((rows, cols), f32),
                vm((rows, cols), f32),
                dma((6,)), dma((half,)), dma((half,)), dma((half,)), dma((half,)),
                dma((n,)), dma((n,)), dma((n,)), dma((n,)), dma((4,)), dma((4,)),
            ],
            compiler_params=pltpu.CompilerParams(
                collective_id=0, has_side_effects=True, vmem_limit_bytes=56 * 2**20
            ),
        )(dataset, centers, weights, batch_index, targets, gamma)
        return pl.pallas_call(
            hand_over,
            out_shape=outs,
            in_specs=[anywhere] * 2,
            out_specs=(anywhere, anywhere),
            scratch_shapes=[dma((2,))],
            compiler_params=pltpu.CompilerParams(vmem_limit_bytes=60 * 2**20),
        )(*results)

    return jax.shard_map(
        per_device,
        mesh=mesh,
        in_specs=(
            P(("groups", "center", "row"), None),
            P(("groups", "center"), None),
            P(("groups", "center"), "row"),
            P(None, ("groups", "center", "row")),
            P(None, ("groups", "center", "row"), None),
            P("groups"),
        ),
        out_specs=(P(("groups", "center"), "row"), P(("groups", "center", "row"), None)),
        check_vma=False,
    )
```

```python
import functools

import jax
import jax.numpy as jnp
from jax import lax
from jax.experimental import pallas as pl
from jax.experimental.pallas import tpu as pltpu
from jax.sharding import PartitionSpec as P

MESH = pl.DeviceIdType.MESH
LANES = 128
NN = (((1,), (0,)), ((), ()))
NT = (((1,), (1,)), ((), ()))
UNROLL = 8


def split(v):
    hi = v.astype(jnp.bfloat16)
    return hi, (v - hi.astype(jnp.float32)).astype(jnp.bfloat16)


def dot3(a, b, dims=NN):
    (ah, al), (bh, bl) = a, b
    dot = functools.partial(lax.dot_general, dimension_numbers=dims, preferred_element_type=jnp.float32)
    return dot(ah, bh) + (dot(ah, bl) + dot(al, bh))


def each(lo, hi, body):
    if hi - lo <= UNROLL:
        for d in range(lo, hi):
            body(d)
    else:
        lax.fori_loop(lo, hi, lambda d, _: (body(d), 0)[1], 0)


def kernel(
    n, ds_hbm, cen_hbm, w_hbm, idx_hbm, tgt_hbm, gam_ref, w_out, res_out,
    ds_ref, cen_ref, w_ref, idx_ref, tgt_ref,
    xbuf, kbuf, tsib, tplace, part, rs_in, allv, res_s, rsend, rrecv,
    in_s, x_ss, x_rs, f_ss, f_rs, p_ss, p_rs, a_ss, a_rs, s_ss, s_rs,
):
    f32 = jnp.float32
    c, r = lax.axis_index("center"), lax.axis_index("row")
    sib = 1 - r
    half = n // 2
    h, side = c // 2, lax.rem(c, 2)
    place = side * half + h
    steps, rows = idx_ref.shape
    slot = steps * rows
    chunks = 2 * n
    batch = rows * chunks
    cols = w_ref.shape[1]
    ncen = cen_ref.shape[0]
    rate = 0.5 / batch
    fold, rp, rg, pw, gw = sizes(n, batch, steps, cols)

    ins = [
        pltpu.make_async_copy(src, dst, in_s.at[i])
        for i, (src, dst) in enumerate(
            [(idx_hbm, idx_ref), (ds_hbm, ds_ref), (tgt_hbm, tgt_ref), (cen_hbm, cen_ref), (w_hbm, w_ref)]
        )
    ]
    for one in ins:
        one.start()

    barrier = pltpu.get_barrier_semaphore()

    def to(d):
        return {"center": lax.rem(c + d, n), "row": r}

    to_sib = {"center": c, "row": sib}
    to_pair = {"center": 2 * h + 1 - side, "row": r}
    each(1, n, lambda d: pl.semaphore_signal(barrier, inc=1, device_id=to(d), device_id_type=MESH))
    pl.semaphore_signal(barrier, inc=1, device_id=to_sib, device_id_type=MESH)

    def copy(src, dst, ss, rs, peer):
        return pltpu.make_async_remote_copy(
            src_ref=src, dst_ref=dst, send_sem=ss, recv_sem=rs, device_id=peer, device_id_type=MESH
        )

    ins[0].wait()
    ins[1].wait()
    for b in range(steps):
        for i in range(rows):
            xbuf[place, pl.ds(b * rows + i, 1), :] = ds_ref[pl.ds(idx_ref[b, i], 1), :]
    ins[2].wait()

    pl.semaphore_wait(barrier, n)

    def x_copy(e):
        peer = {"center": 2 * lax.rem(h + e, half) + side, "row": r}
        return copy(xbuf.at[place], xbuf.at[place], x_ss.at[e], x_rs.at[e], peer)

    def f_copy(e):
        at = side * half + lax.rem(h + half - e, half)
        return copy(xbuf.at[at], xbuf.at[at], f_ss.at[e], f_rs.at[e], to_pair)

    each(1, half, lambda e: x_copy(e).start())
    f_copy(0).start()
    sib_cols = pl.ds(pl.multiple_of(sib * cols, LANES), cols)
    own_cols = pl.ds(pl.multiple_of(r * cols, LANES), cols)
    t_copy = copy(tgt_ref.at[:, :, sib_cols], tsib, s_ss.at[0], s_rs.at[0], to_sib)
    t_copy.start()

    ins[3].wait()
    cen = cen_ref[...]
    cen2 = split(cen)
    csq = jnp.sum(cen * cen, axis=1, keepdims=True)
    csq = jnp.transpose(jnp.broadcast_to(csq, (ncen, ncen)))[0:1, :]
    ins[4].wait()
    w2 = split(w_ref[...])
    gamma = gam_ref[0]

    def pass_on(e):
        x_copy(e).wait_recv()
        f_copy(e).start()

    each(1, half, pass_on)

    count = half * slot
    step = min(count, UNROLL * slot)

    def kernel_rows(which, s):
        first = pl.multiple_of(which * count + s * step, slot)
        x = xbuf[pl.ds(which * half + s * (step // slot), step // slot)].reshape(step, xbuf.shape[2])
        xsq = jnp.sum(x * x, axis=1, keepdims=True)
        cross = dot3(split(x), cen2, NT)
        kbuf[pl.ds(pl.multiple_of(r * (n * slot) + first, slot), step), :] = jnp.exp(
            -gamma * (xsq + csq - 2.0 * cross)
        )

    def k_copy(i, which):
        at = pl.ds(pl.multiple_of(r * (n * slot) + which * count, slot), count)
        return copy(kbuf.at[at, :], kbuf.at[at, :], s_ss.at[i], s_rs.at[i], to_sib)

    each(0, count // step, lambda s: kernel_rows(side, s))
    k_copy(1, side).start()

    t_copy.wait()
    chunk_id = lax.broadcasted_iota(jnp.int32, (chunks, cols), 0)
    for b in range(steps):
        mine, other = tgt_ref[b, :, own_cols], tsib[b]
        for i in range(rows):
            j = b * rows + i
            placed = jnp.where(chunk_id == r * n + place, mine[i : i + 1, :], 0.0)
            placed = jnp.where(chunk_id == sib * n + place, other[i : i + 1, :], placed)
            tplace[pl.ds(j * chunks, chunks), :] = placed

    each(0, half, lambda e: f_copy(e).wait_recv())
    each(0, count // step, lambda s: kernel_rows(1 - side, s))
    k_copy(2, 1 - side).start()
    k_copy(1, side).wait()
    k_copy(2, 1 - side).wait()

    k_all = jnp.concatenate([kbuf[pl.ds(j, chunks, stride=slot), :] for j in range(slot)], axis=0)
    kh, kl = split(k_all)
    k0 = (jnp.concatenate([kh[:batch]] * fold, axis=0), jnp.concatenate([kl[:batch]] * fold, axis=0))

    blocks = max(1, n // UNROLL)
    per = n // blocks
    for s in range(blocks):
        lo, hi = s * per * rp, (s + 1) * per * rp
        p = dot3((kh[lo:hi], kl[lo:hi]), w2) - tplace[lo:hi, :]
        lo, hi = batch + s * per * rg * fold, batch + (s + 1) * per * rg * fold
        g = fold_rows(dot3((kh[lo:hi], kl[lo:hi]), k0, NT), fold, batch)
        for o in range(per):
            for l in range(pw):
                part[s * per + o, l * rp : (l + 1) * rp, :] = p[o * rp : (o + 1) * rp, l * LANES : (l + 1) * LANES]
            for l in range(gw):
                at = pw * rp + l * rg
                part[s * per + o, at : at + rg, :] = g[o * rg : (o + 1) * rg, l * LANES : (l + 1) * LANES]

    def p_copy(d):
        return copy(part.at[lax.rem(c + d, n)], rs_in.at[d], p_ss.at[d], p_rs.at[d], to(d))

    each(1, n, lambda d: p_copy(d).start())
    k_t = split(jnp.transpose(k_all))
    allv[c] = part[c]

    def add(d):
        p_copy(d).wait_recv()
        allv[c] += rs_in[d]

    each(1, n, add)

    def a_copy(d):
        return copy(allv.at[c], allv.at[c], a_ss.at[d], a_rs.at[d], to(d))

    each(1, n, lambda d: a_copy(d).start())
    each(1, n, lambda d: a_copy(d).wait_recv())

    def whole(at, size, width):
        pieces = [
            jnp.concatenate([allv[o, at + l * size : at + (l + 1) * size, :] for o in range(n)], axis=0)
            for l in range(width)
        ]
        return pieces[0] if width == 1 else jnp.concatenate(pieces, axis=1)

    a = whole(0, rp, pw)
    g = unfold_rows(whole(pw * rp, rg, gw), fold, batch)
    res0 = a[:batch]
    res0h, res0l = split(res0)
    res0f = (jnp.concatenate([res0h] * fold, axis=0), jnp.concatenate([res0l] * fold, axis=0))
    res1 = a[batch:] - rate * dot3(split(g), res0f)
    res_s[...] = res1
    for i in range(rows):
        rsend[i : i + 1, :] = res_s[pl.ds(i * chunks + sib * n + place, 1), :]
    r_copy = copy(rsend, rrecv, s_ss.at[3], s_rs.at[3], to_sib)
    r_copy.start()
    for i in range(rows):
        res_out[i : i + 1, own_cols] = res_s[pl.ds(i * chunks + r * n + place, 1), :]
    res1h, res1l = split(res1)
    res = (jnp.concatenate([res0h, res1h], axis=0), jnp.concatenate([res0l, res1l], axis=0))
    w_out[...] = w_ref[...] - rate * dot3(k_t, res)
    r_copy.wait()
    res_out[:, sib_cols] = rrecv[...]

    def drain(d):
        p_copy(d).wait_send()
        a_copy(d).wait_send()

    each(1, n, drain)
    each(1, half, lambda e: x_copy(e).wait_send())
    each(0, half, lambda e: f_copy(e).wait_send())


def sizes(n, batch, steps, cols):
    fold = max(1, LANES // batch)
    return fold, steps * batch // n, batch // fold // n, cols // LANES, pl.cdiv(batch, LANES)


def fold_rows(g, fold, batch):
    if fold == 1:
        return g
    height = g.shape[0] // fold
    at = lax.broadcasted_iota(jnp.int32, (height, LANES), 1) // batch
    out = g[:height]
    for f in range(1, fold):
        out = jnp.where(at == f, g[f * height : (f + 1) * height], out)
    return out


def unfold_rows(g, fold, batch):
    if fold == 1:
        return g
    at = lax.broadcasted_iota(jnp.int32, g.shape, 1) // batch
    return jnp.concatenate([jnp.where(at == f, g, 0.0) for f in range(fold)], axis=0)


def hand_over(w_in, res_in, w_out, res_out, sems):
    copies = [
        pltpu.make_async_copy(w_in, w_out, sems.at[0]),
        pltpu.make_async_copy(res_in, res_out, sems.at[1]),
    ]
    for one in copies:
        one.start()
    for one in copies:
        one.wait()


def solution(mesh):
    n = mesh.shape["center"]

    def per_device(dataset, centers, weights, batch_index, targets, gamma):
        f32 = jnp.float32
        steps, rows = batch_index.shape
        slot, feats = steps * rows, dataset.shape[1]
        ncen, cols = weights.shape
        total, batch = slot * 2 * n, rows * 2 * n
        fold, rp, rg, pw, gw = sizes(n, batch, steps, cols)
        height = pw * rp + gw * rg
        half = n // 2
        vm = pltpu.VMEM
        dma = pltpu.SemaphoreType.DMA
        anywhere = pl.BlockSpec(memory_space=pltpu.HBM)
        outs = (
            jax.ShapeDtypeStruct(weights.shape, f32),
            jax.ShapeDtypeStruct(targets.shape[1:], f32),
        )
        results = pl.pallas_call(
            functools.partial(kernel, n),
            out_shape=outs,
            in_specs=[anywhere] * 5 + [pl.BlockSpec(memory_space=pltpu.SMEM)],
            out_specs=(pl.BlockSpec(memory_space=pltpu.VMEM), pl.BlockSpec(memory_space=pltpu.VMEM)),
            scratch_shapes=[
                vm(dataset.shape, f32), vm(centers.shape, f32), vm(weights.shape, f32),
                pltpu.SMEM(batch_index.shape, jnp.int32), vm(targets.shape, f32),
                vm((n, slot, feats), f32),
                vm((2 * n * slot, ncen), f32),
                vm((steps, rows, cols), f32),
                vm((total, cols), f32),
                vm((n, height, LANES), f32),
                vm((n, height, LANES), f32),
                vm((n, height, LANES), f32),
                vm((batch, cols), f32),
                vm((rows, cols), f32),
                vm((rows, cols), f32),
                dma((5,)), dma((half,)), dma((half,)), dma((half,)), dma((half,)),
                dma((n,)), dma((n,)), dma((n,)), dma((n,)), dma((4,)), dma((4,)),
            ],
            compiler_params=pltpu.CompilerParams(
                collective_id=0, has_side_effects=True, vmem_limit_bytes=min(56, 8 + 3 * n) * 2**20
            ),
        )(*[
            pltpu.with_memory_space_constraint(v, pltpu.HBM)
            for v in (dataset, centers, weights, batch_index, targets)
        ], gamma)
        return pl.pallas_call(
            hand_over,
            out_shape=outs,
            in_specs=[pl.BlockSpec(memory_space=pltpu.VMEM)] * 2,
            out_specs=(anywhere, anywhere),
            scratch_shapes=[dma((2,))],
            compiler_params=pltpu.CompilerParams(vmem_limit_bytes=4 * 2**20),
        )(*results)

    return jax.shard_map(
        per_device,
        mesh=mesh,
        in_specs=(
            P(("groups", "center", "row"), None),
            P(("groups", "center"), None),
            P(("groups", "center"), "row"),
            P(None, ("groups", "center", "row")),
            P(None, ("groups", "center", "row"), None),
            P("groups"),
        ),
        out_specs=(P(("groups", "center"), "row"), P(("groups", "center", "row"), None)),
        check_vma=False,
    )
```

```python
import functools

import jax
import jax.numpy as jnp
from jax import lax
from jax.experimental import pallas as pl
from jax.experimental.pallas import tpu as pltpu
from jax.sharding import PartitionSpec as P

MESH = pl.DeviceIdType.MESH
LANES = 128
NN = (((1,), (0,)), ((), ()))
NT = (((1,), (1,)), ((), ()))
UNROLL = 8


def split(v):
    hi = v.astype(jnp.bfloat16)
    return hi, (v - hi.astype(jnp.float32)).astype(jnp.bfloat16)


def dot3(a, b, dims=NN):
    (ah, al), (bh, bl) = a, b
    dot = functools.partial(lax.dot_general, dimension_numbers=dims, preferred_element_type=jnp.float32)
    both = dot(jnp.concatenate([ah, al], axis=0), bh)
    height = ah.shape[0]
    return both[:height] + (dot(ah, bl) + both[height:])


def each(lo, hi, body):
    if hi - lo <= UNROLL:
        for d in range(lo, hi):
            body(d)
    else:
        lax.fori_loop(lo, hi, lambda d, _: (body(d), 0)[1], 0)


def kernel(
    n, ds_hbm, cen_hbm, w_hbm, idx_hbm, tgt_hbm, gam_ref, w_out, res_out,
    ds_ref, cen_ref, w_ref, idx_ref, tgt_ref,
    xbuf, kbuf, tsib, tplace, part, rs_in, partq, rs_inq, allv, res_s, rsend, rrecv,
    in_s, x_ss, x_rs, f_ss, f_rs, p_ss, p_rs, q_ss, q_rs, a_ss, a_rs, s_ss, s_rs,
):
    f32 = jnp.float32
    c, r = lax.axis_index("center"), lax.axis_index("row")
    sib = 1 - r
    half = n // 2
    h, side = c // 2, lax.rem(c, 2)
    place = side * half + h
    steps, rows = idx_ref.shape
    slot = steps * rows
    batch = 2 * rows * n
    cols = w_ref.shape[1]
    ncen = cen_ref.shape[0]
    rate = 0.5 / batch
    fold, rg, pw, gw = sizes(n, batch, cols)

    ins = [
        pltpu.make_async_copy(src, dst, in_s.at[i])
        for i, (src, dst) in enumerate(
            [(idx_hbm, idx_ref), (ds_hbm, ds_ref), (tgt_hbm, tgt_ref), (cen_hbm, cen_ref), (w_hbm, w_ref)]
        )
    ]
    for one in ins:
        one.start()

    barrier = pltpu.get_barrier_semaphore()

    def to(d):
        return {"center": lax.rem(c + d, n), "row": r}

    to_sib = {"center": c, "row": sib}
    to_pair = {"center": 2 * h + 1 - side, "row": r}
    each(1, n, lambda d: pl.semaphore_signal(barrier, inc=1, device_id=to(d), device_id_type=MESH))
    pl.semaphore_signal(barrier, inc=1, device_id=to_sib, device_id_type=MESH)

    def copy(src, dst, ss, rs, peer):
        return pltpu.make_async_remote_copy(
            src_ref=src, dst_ref=dst, send_sem=ss, recv_sem=rs, device_id=peer, device_id_type=MESH
        )

    ins[0].wait()
    ins[1].wait()
    for b in range(steps):
        for i in range(rows):
            xbuf[place, pl.ds(b * rows + i, 1), :] = ds_ref[pl.ds(idx_ref[b, i], 1), :]
    ins[2].wait()

    pl.semaphore_wait(barrier, n)

    def x_copy(e):
        peer = {"center": 2 * lax.rem(h + e, half) + side, "row": r}
        return copy(xbuf.at[place], xbuf.at[place], x_ss.at[e], x_rs.at[e], peer)

    def f_copy(e):
        at = side * half + lax.rem(h + half - e, half)
        return copy(xbuf.at[at], xbuf.at[at], f_ss.at[e], f_rs.at[e], to_pair)

    each(1, half, lambda e: x_copy(e).start())
    f_copy(0).start()
    sib_cols = pl.ds(pl.multiple_of(sib * cols, LANES), cols)
    own_cols = pl.ds(pl.multiple_of(r * cols, LANES), cols)
    t_copy = copy(tgt_ref.at[:, :, sib_cols], tsib, s_ss.at[0], s_rs.at[0], to_sib)
    t_copy.start()

    ins[3].wait()
    cen = cen_ref[...]
    cen2 = split(cen)
    csq = jnp.sum(cen * cen, axis=1, keepdims=True)
    csq = jnp.transpose(jnp.broadcast_to(csq, (ncen, ncen)))[0:1, :]
    ins[4].wait()
    w2 = split(w_ref[...])
    gamma = gam_ref[0]

    def pass_on(e):
        x_copy(e).wait_recv()
        f_copy(e).start()

    each(1, half, pass_on)

    count = half * slot
    step = min(count, UNROLL * slot)

    def kernel_rows(which, s):
        first = pl.multiple_of(which * count + s * step, slot)
        x = xbuf[pl.ds(which * half + s * (step // slot), step // slot)].reshape(step, xbuf.shape[2])
        xsq = jnp.sum(x * x, axis=1, keepdims=True)
        cross = dot3(split(x), cen2, NT)
        kbuf[pl.ds(pl.multiple_of(r * (n * slot) + first, slot), step), :] = jnp.exp(
            -gamma * (xsq + csq - 2.0 * cross)
        )

    def k_copy(i, which):
        at = pl.ds(pl.multiple_of(r * (n * slot) + which * count, slot), count)
        return copy(kbuf.at[at, :], kbuf.at[at, :], s_ss.at[i], s_rs.at[i], to_sib)

    each(0, count // step, lambda s: kernel_rows(side, s))
    k_copy(1, side).start()

    t_copy.wait()
    place_id = lax.broadcasted_iota(jnp.int32, (n, cols), 0)
    for j in range(slot):
        b, i = divmod(j, rows)
        tplace[0, j * n : (j + 1) * n, :] = jnp.where(place_id == place, tgt_ref[b, i : i + 1, own_cols], 0.0)
        tplace[1, j * n : (j + 1) * n, :] = jnp.where(place_id == place, tsib[b, i : i + 1, :], 0.0)

    each(0, half, lambda e: f_copy(e).wait_recv())
    each(0, count // step, lambda s: kernel_rows(1 - side, s))
    k_copy(2, 1 - side).start()

    def core_rows(core):
        return jnp.concatenate(
            [kbuf[pl.ds(core * (n * slot) + j, n, stride=slot), :] for j in range(slot)], axis=0
        )

    def predict(core, which):
        return dot3(split(core_rows(core)), w2) - tplace[which]

    def put(ref, values, at, size):
        for l in range(values.shape[1] // LANES):
            for o in range(n):
                ref[o, at + l * size : at + (l + 1) * size, :] = values[
                    o * size : (o + 1) * size, l * LANES : (l + 1) * LANES
                ]

    def p_copy(d):
        return copy(part.at[lax.rem(c + d, n)], rs_in.at[d], p_ss.at[d], p_rs.at[d], to(d))

    def q_copy(d):
        return copy(partq.at[lax.rem(c + d, n)], rs_inq.at[d], q_ss.at[d], q_rs.at[d], to(d))

    put(part, predict(r, 0), 0, slot)
    each(1, n, lambda d: p_copy(d).start())

    k_copy(1, side).wait()
    k_copy(2, 1 - side).wait()
    put(partq, predict(sib, 1), 0, slot)
    kernels = [core_rows(core) for core in range(2)]
    k_0 = jnp.concatenate([v[: rows * n] for v in kernels], axis=0)
    k_1 = jnp.concatenate([v[rows * n :] for v in kernels], axis=0)
    k0h, k0l = split(k_0)
    k0f = (jnp.concatenate([k0h] * fold, axis=0), jnp.concatenate([k0l] * fold, axis=0))
    put(partq, fold_rows(dot3(split(k_1), k0f, NT), fold, batch), pw * slot, rg)
    each(1, n, lambda d: q_copy(d).start())

    k_t = split(jnp.transpose(jnp.concatenate([k_0, k_1], axis=0)))
    core_at = [pl.multiple_of(core * (pw * slot), slot) for core in (r, sib)]
    own_at, sib_at = (pl.ds(at, pw * slot) for at in core_at)
    g_at = pl.ds(2 * pw * slot, gw * rg)
    q_at, qg_at = pl.ds(0, pw * slot), pl.ds(pw * slot, gw * rg)
    allv[c, own_at, :] = part[c]
    allv[c, sib_at, :] = partq[c, q_at, :]
    allv[c, g_at, :] = partq[c, qg_at, :]

    def add(d):
        p_copy(d).wait_recv()
        allv[c, own_at, :] += rs_in[d]

    def addq(d):
        q_copy(d).wait_recv()
        allv[c, sib_at, :] += rs_inq[d, q_at, :]
        allv[c, g_at, :] += rs_inq[d, qg_at, :]

    each(1, n, add)
    each(1, n, addq)

    def a_copy(d):
        return copy(allv.at[c], allv.at[c], a_ss.at[d], a_rs.at[d], to(d))

    each(1, n, lambda d: a_copy(d).start())
    each(1, n, lambda d: a_copy(d).wait_recv())

    def take(at, size, width, owners):
        pieces = [
            jnp.concatenate([allv[o, at + l * size : at + (l + 1) * size, :] for o in owners], axis=0)
            for l in range(width)
        ]
        return pieces[0] if width == 1 else jnp.concatenate(pieces, axis=1)

    def both_cores(owners):
        return jnp.concatenate([take(core * (pw * slot), slot, pw, owners) for core in range(2)], axis=0)

    g = unfold_rows(take(2 * pw * slot, rg, gw, range(n)), fold, batch)
    res0h, res0l = split(both_cores(range(n // 2)))
    res0f = (jnp.concatenate([res0h] * fold, axis=0), jnp.concatenate([res0l] * fold, axis=0))
    res1 = both_cores(range(n // 2, n)) - rate * dot3(split(g), res0f)
    res_s[...] = res1
    for i in range(rows):
        rsend[i : i + 1, :] = res_s[pl.ds((sib * rows + i) * n + place, 1), :]
    r_copy = copy(rsend, rrecv, s_ss.at[3], s_rs.at[3], to_sib)
    r_copy.start()
    for i in range(rows):
        res_out[i : i + 1, own_cols] = res_s[pl.ds((r * rows + i) * n + place, 1), :]
    res1h, res1l = split(res1)
    res = (jnp.concatenate([res0h, res1h], axis=0), jnp.concatenate([res0l, res1l], axis=0))
    w_out[...] = w_ref[...] - rate * dot3(k_t, res)
    r_copy.wait()
    res_out[:, sib_cols] = rrecv[...]

    def drain(d):
        p_copy(d).wait_send()
        q_copy(d).wait_send()
        a_copy(d).wait_send()

    each(1, n, drain)
    each(1, half, lambda e: x_copy(e).wait_send())
    each(0, half, lambda e: f_copy(e).wait_send())


def sizes(n, batch, cols):
    fold = max(1, LANES // batch)
    return fold, batch // fold // n, cols // LANES, pl.cdiv(batch, LANES)


def fold_rows(g, fold, batch):
    if fold == 1:
        return g
    height = g.shape[0] // fold
    at = lax.broadcasted_iota(jnp.int32, (height, LANES), 1) // batch
    out = g[:height]
    for f in range(1, fold):
        out = jnp.where(at == f, g[f * height : (f + 1) * height], out)
    return out


def unfold_rows(g, fold, batch):
    if fold == 1:
        return g
    at = lax.broadcasted_iota(jnp.int32, g.shape, 1) // batch
    return jnp.concatenate([jnp.where(at == f, g, 0.0) for f in range(fold)], axis=0)


def hand_over(w_in, res_in, w_out, res_out, sems):
    copies = [
        pltpu.make_async_copy(w_in, w_out, sems.at[0]),
        pltpu.make_async_copy(res_in, res_out, sems.at[1]),
    ]
    for one in copies:
        one.start()
    for one in copies:
        one.wait()


def solution(mesh):
    n = mesh.shape["center"]

    def per_device(dataset, centers, weights, batch_index, targets, gamma):
        f32 = jnp.float32
        steps, rows = batch_index.shape
        slot, feats = steps * rows, dataset.shape[1]
        ncen, cols = weights.shape
        total, batch = slot * 2 * n, rows * 2 * n
        fold, rg, pw, gw = sizes(n, batch, cols)
        height, extra = pw * slot, gw * rg
        half = n // 2
        vm = pltpu.VMEM
        dma = pltpu.SemaphoreType.DMA
        anywhere = pl.BlockSpec(memory_space=pltpu.HBM)
        outs = (
            jax.ShapeDtypeStruct(weights.shape, f32),
            jax.ShapeDtypeStruct(targets.shape[1:], f32),
        )
        results = pl.pallas_call(
            functools.partial(kernel, n),
            out_shape=outs,
            in_specs=[anywhere] * 5 + [pl.BlockSpec(memory_space=pltpu.SMEM)],
            out_specs=(pl.BlockSpec(memory_space=pltpu.VMEM), pl.BlockSpec(memory_space=pltpu.VMEM)),
            scratch_shapes=[
                vm(dataset.shape, f32), vm(centers.shape, f32), vm(weights.shape, f32),
                pltpu.SMEM(batch_index.shape, jnp.int32), vm(targets.shape, f32),
                vm((n, slot, feats), f32),
                vm((2 * n * slot, ncen), f32),
                vm((steps, rows, cols), f32),
                vm((2, total // 2, cols), f32),
                vm((n, height, LANES), f32),
                vm((n, height, LANES), f32),
                vm((n, height + extra, LANES), f32),
                vm((n, height + extra, LANES), f32),
                vm((n, 2 * height + extra, LANES), f32),
                vm((batch, cols), f32),
                vm((rows, cols), f32),
                vm((rows, cols), f32),
                dma((5,)), dma((half,)), dma((half,)), dma((half,)), dma((half,)),
                dma((n,)), dma((n,)), dma((n,)), dma((n,)), dma((n,)), dma((n,)), dma((4,)), dma((4,)),
            ],
            compiler_params=pltpu.CompilerParams(
                collective_id=0, has_side_effects=True, vmem_limit_bytes=min(56, 8 + 3 * n) * 2**20
            ),
        )(*[
            pltpu.with_memory_space_constraint(v, pltpu.HBM)
            for v in (dataset, centers, weights, batch_index, targets)
        ], gamma)
        return pl.pallas_call(
            hand_over,
            out_shape=outs,
            in_specs=[pl.BlockSpec(memory_space=pltpu.VMEM)] * 2,
            out_specs=(anywhere, anywhere),
            scratch_shapes=[dma((2,))],
            compiler_params=pltpu.CompilerParams(vmem_limit_bytes=4 * 2**20),
        )(*results)

    return jax.shard_map(
        per_device,
        mesh=mesh,
        in_specs=(
            P(("groups", "center", "row"), None),
            P(("groups", "center"), None),
            P(("groups", "center"), "row"),
            P(None, ("groups", "center", "row")),
            P(None, ("groups", "center", "row"), None),
            P("groups"),
        ),
        out_specs=(P(("groups", "center"), "row"), P(("groups", "center", "row"), None)),
        check_vma=False,
    )
```

```python
import functools

import jax
import jax.numpy as jnp
from jax import lax
from jax.experimental import pallas as pl
from jax.experimental.pallas import tpu as pltpu
from jax.sharding import PartitionSpec as P

MESH = pl.DeviceIdType.MESH
LANES = 128
NN = (((1,), (0,)), ((), ()))
NT = (((1,), (1,)), ((), ()))
UNROLL = 8


def split(v):
    hi = v.astype(jnp.bfloat16)
    return hi, (v - hi.astype(jnp.float32)).astype(jnp.bfloat16)


def dot3(a, b, dims=NN):
    (ah, al), (bh, bl) = a, b
    dot = functools.partial(lax.dot_general, dimension_numbers=dims, preferred_element_type=jnp.float32)
    both = dot(jnp.concatenate([ah, al], axis=0), bh)
    height = ah.shape[0]
    return both[:height] + (dot(ah, bl) + both[height:])


def each(lo, hi, body):
    if hi - lo <= UNROLL:
        for d in range(lo, hi):
            body(d)
    else:
        lax.fori_loop(lo, hi, lambda d, _: (body(d), 0)[1], 0)


def kernel(
    n, ds_hbm, cen_hbm, w_hbm, idx_hbm, tgt_hbm, gam_ref, w_out, res_out,
    ds_ref, cen_ref, w_ref, idx_ref, tgt_ref,
    xbuf, kbuf, tsib, tplace, part, rs_in, partq, rs_inq, sums, sumsq, res_s, rsend, rrecv,
    in_s, x_ss, x_rs, f_ss, f_rs, p_ss, p_rs, q_ss, q_rs, a_ss, a_rs, b_ss, b_rs, s_ss, s_rs,
):
    f32 = jnp.float32
    c, r = lax.axis_index("center"), lax.axis_index("row")
    sib = 1 - r
    half = n // 2
    h, side = c // 2, lax.rem(c, 2)
    place = side * half + h
    steps, rows = idx_ref.shape
    slot = steps * rows
    batch = 2 * rows * n
    cols = w_ref.shape[1]
    ncen = cen_ref.shape[0]
    rate = 0.5 / batch
    fold, rg, pw, gw = sizes(n, batch, cols)

    ins = [
        pltpu.make_async_copy(src, dst, in_s.at[i])
        for i, (src, dst) in enumerate(
            [(idx_hbm, idx_ref), (ds_hbm, ds_ref), (tgt_hbm, tgt_ref), (cen_hbm, cen_ref), (w_hbm, w_ref)]
        )
    ]
    for one in ins:
        one.start()

    barrier = pltpu.get_barrier_semaphore()

    def to(d):
        return {"center": lax.rem(c + d, n), "row": r}

    to_sib = {"center": c, "row": sib}
    to_pair = {"center": 2 * h + 1 - side, "row": r}
    each(1, n, lambda d: pl.semaphore_signal(barrier, inc=1, device_id=to(d), device_id_type=MESH))
    pl.semaphore_signal(barrier, inc=1, device_id=to_sib, device_id_type=MESH)

    def copy(src, dst, ss, rs, peer):
        return pltpu.make_async_remote_copy(
            src_ref=src, dst_ref=dst, send_sem=ss, recv_sem=rs, device_id=peer, device_id_type=MESH
        )

    ins[0].wait()
    ins[1].wait()
    for b in range(steps):
        for i in range(rows):
            xbuf[place, pl.ds(b * rows + i, 1), :] = ds_ref[pl.ds(idx_ref[b, i], 1), :]
    ins[2].wait()

    pl.semaphore_wait(barrier, n)

    def x_copy(e):
        peer = {"center": 2 * lax.rem(h + e, half) + side, "row": r}
        return copy(xbuf.at[place], xbuf.at[place], x_ss.at[e], x_rs.at[e], peer)

    def f_copy(e):
        at = side * half + lax.rem(h + half - e, half)
        return copy(xbuf.at[at], xbuf.at[at], f_ss.at[e], f_rs.at[e], to_pair)

    each(1, half, lambda e: x_copy(e).start())
    f_copy(0).start()
    sib_cols = pl.ds(pl.multiple_of(sib * cols, LANES), cols)
    own_cols = pl.ds(pl.multiple_of(r * cols, LANES), cols)
    t_copy = copy(tgt_ref.at[:, :, sib_cols], tsib, s_ss.at[0], s_rs.at[0], to_sib)
    t_copy.start()

    ins[3].wait()
    cen = cen_ref[...]
    cen2 = split(cen)
    csq = jnp.sum(cen * cen, axis=1, keepdims=True)
    csq = jnp.transpose(jnp.broadcast_to(csq, (ncen, ncen)))[0:1, :]
    ins[4].wait()
    w2 = split(w_ref[...])
    gamma = gam_ref[0]

    def pass_on(e):
        x_copy(e).wait_recv()
        f_copy(e).start()

    each(1, half, pass_on)

    count = half * slot
    step = min(count, UNROLL * slot)

    def kernel_rows(which, s):
        first = pl.multiple_of(which * count + s * step, slot)
        x = xbuf[pl.ds(which * half + s * (step // slot), step // slot)].reshape(step, xbuf.shape[2])
        xsq = jnp.sum(x * x, axis=1, keepdims=True)
        cross = dot3(split(x), cen2, NT)
        kbuf[pl.ds(pl.multiple_of(r * (n * slot) + first, slot), step), :] = jnp.exp(
            -gamma * (xsq + csq - 2.0 * cross)
        )

    def k_copy(i, which):
        at = pl.ds(pl.multiple_of(r * (n * slot) + which * count, slot), count)
        return copy(kbuf.at[at, :], kbuf.at[at, :], s_ss.at[i], s_rs.at[i], to_sib)

    each(0, count // step, lambda s: kernel_rows(side, s))
    k_copy(1, side).start()

    t_copy.wait()
    place_id = lax.broadcasted_iota(jnp.int32, (n, cols), 0)
    for j in range(slot):
        b, i = divmod(j, rows)
        tplace[0, j * n : (j + 1) * n, :] = jnp.where(place_id == place, tgt_ref[b, i : i + 1, own_cols], 0.0)
        tplace[1, j * n : (j + 1) * n, :] = jnp.where(place_id == place, tsib[b, i : i + 1, :], 0.0)

    each(0, half, lambda e: f_copy(e).wait_recv())
    each(0, count // step, lambda s: kernel_rows(1 - side, s))
    k_copy(2, 1 - side).start()

    def core_rows(core):
        return jnp.concatenate(
            [kbuf[pl.ds(core * (n * slot) + j, n, stride=slot), :] for j in range(slot)], axis=0
        )

    def predict(which):
        return dot3(split(kernels[which]), w2) - tplace[which]

    def put(ref, values, at, size):
        for l in range(values.shape[1] // LANES):
            for o in range(n):
                ref[o, at + l * size : at + (l + 1) * size, :] = values[
                    o * size : (o + 1) * size, l * LANES : (l + 1) * LANES
                ]

    def p_copy(d):
        return copy(part.at[lax.rem(c + d, n)], rs_in.at[d], p_ss.at[d], p_rs.at[d], to(d))

    def q_copy(d):
        return copy(partq.at[lax.rem(c + d, n)], rs_inq.at[d], q_ss.at[d], q_rs.at[d], to(d))

    kernels = [core_rows(r)]
    put(part, predict(0), 0, slot)
    each(1, n, lambda d: p_copy(d).start())

    k_copy(1, side).wait()
    k_copy(2, 1 - side).wait()
    kernels.append(core_rows(sib))
    put(partq, predict(1), 0, slot)
    k_0 = jnp.concatenate([v[: rows * n] for v in kernels], axis=0)
    k_1 = jnp.concatenate([v[rows * n :] for v in kernels], axis=0)
    k0h, k0l = split(k_0)
    k0f = (jnp.concatenate([k0h] * fold, axis=0), jnp.concatenate([k0l] * fold, axis=0))
    put(partq, fold_rows(dot3(split(k_1), k0f, NT), fold, batch), pw * slot, rg)
    each(1, n, lambda d: q_copy(d).start())

    k_t = split(jnp.transpose(jnp.concatenate([k_0, k_1], axis=0)))
    sums[c] = part[c]
    sumsq[c] = partq[c]

    def add(d):
        p_copy(d).wait_recv()
        sums[c] += rs_in[d]

    def addq(d):
        q_copy(d).wait_recv()
        sumsq[c] += rs_inq[d]

    def a_copy(d):
        return copy(sums.at[c], sums.at[c], a_ss.at[d], a_rs.at[d], to(d))

    def b_copy(d):
        return copy(sumsq.at[c], sumsq.at[c], b_ss.at[d], b_rs.at[d], to(d))

    each(1, n, add)
    each(1, n, lambda d: a_copy(d).start())
    each(1, n, addq)
    each(1, n, lambda d: b_copy(d).start())
    each(1, n, lambda d: a_copy(d).wait_recv())
    each(1, n, lambda d: b_copy(d).wait_recv())

    def take(ref, at, size, width, owners):
        pieces = [
            jnp.concatenate([ref[o, at + l * size : at + (l + 1) * size, :] for o in owners], axis=0)
            for l in range(width)
        ]
        return pieces[0] if width == 1 else jnp.concatenate(pieces, axis=1)

    def both_cores(owners):
        return jnp.concatenate([take(ref, 0, slot, pw, owners) for ref in (sums, sumsq)], axis=0)

    g = unfold_rows(take(sumsq, pw * slot, rg, gw, range(n)), fold, batch)
    res0h, res0l = split(both_cores(range(n // 2)))
    res0f = (jnp.concatenate([res0h] * fold, axis=0), jnp.concatenate([res0l] * fold, axis=0))
    res1 = both_cores(range(n // 2, n)) - rate * dot3(split(g), res0f)
    res_s[...] = res1
    for i in range(rows):
        rsend[i : i + 1, :] = res_s[pl.ds((rows + i) * n + place, 1), :]
    r_copy = copy(rsend, rrecv, s_ss.at[3], s_rs.at[3], to_sib)
    r_copy.start()
    for i in range(rows):
        res_out[i : i + 1, own_cols] = res_s[pl.ds(i * n + place, 1), :]
    res1h, res1l = split(res1)
    res = (jnp.concatenate([res0h, res1h], axis=0), jnp.concatenate([res0l, res1l], axis=0))
    w_out[...] = w_ref[...] - rate * dot3(k_t, res)
    r_copy.wait()
    res_out[:, sib_cols] = rrecv[...]

    def drain(d):
        p_copy(d).wait_send()
        q_copy(d).wait_send()
        a_copy(d).wait_send()
        b_copy(d).wait_send()

    each(1, n, drain)
    each(1, half, lambda e: x_copy(e).wait_send())
    each(0, half, lambda e: f_copy(e).wait_send())


def sizes(n, batch, cols):
    fold = max(1, LANES // batch)
    return fold, batch // fold // n, cols // LANES, pl.cdiv(batch, LANES)


def fold_rows(g, fold, batch):
    if fold == 1:
        return g
    height = g.shape[0] // fold
    at = lax.broadcasted_iota(jnp.int32, (height, LANES), 1) // batch
    out = g[:height]
    for f in range(1, fold):
        out = jnp.where(at == f, g[f * height : (f + 1) * height], out)
    return out


def unfold_rows(g, fold, batch):
    if fold == 1:
        return g
    at = lax.broadcasted_iota(jnp.int32, g.shape, 1) // batch
    return jnp.concatenate([jnp.where(at == f, g, 0.0) for f in range(fold)], axis=0)


def hand_over(w_in, res_in, w_out, res_out, sems):
    copies = [
        pltpu.make_async_copy(w_in, w_out, sems.at[0]),
        pltpu.make_async_copy(res_in, res_out, sems.at[1]),
    ]
    for one in copies:
        one.start()
    for one in copies:
        one.wait()


def solution(mesh):
    n = mesh.shape["center"]

    def per_device(dataset, centers, weights, batch_index, targets, gamma):
        f32 = jnp.float32
        steps, rows = batch_index.shape
        slot, feats = steps * rows, dataset.shape[1]
        ncen, cols = weights.shape
        total, batch = slot * 2 * n, rows * 2 * n
        fold, rg, pw, gw = sizes(n, batch, cols)
        height, extra = pw * slot, gw * rg
        half = n // 2
        vm = pltpu.VMEM
        dma = pltpu.SemaphoreType.DMA
        anywhere = pl.BlockSpec(memory_space=pltpu.HBM)
        outs = (
            jax.ShapeDtypeStruct(weights.shape, f32),
            jax.ShapeDtypeStruct(targets.shape[1:], f32),
        )
        results = pl.pallas_call(
            functools.partial(kernel, n),
            out_shape=outs,
            in_specs=[anywhere] * 5 + [pl.BlockSpec(memory_space=pltpu.SMEM)],
            out_specs=(pl.BlockSpec(memory_space=pltpu.VMEM), pl.BlockSpec(memory_space=pltpu.VMEM)),
            scratch_shapes=[
                vm(dataset.shape, f32), vm(centers.shape, f32), vm(weights.shape, f32),
                pltpu.SMEM(batch_index.shape, jnp.int32), vm(targets.shape, f32),
                vm((n, slot, feats), f32),
                vm((2 * n * slot, ncen), f32),
                vm((steps, rows, cols), f32),
                vm((2, total // 2, cols), f32),
                vm((n, height, LANES), f32),
                vm((n, height, LANES), f32),
                vm((n, height + extra, LANES), f32),
                vm((n, height + extra, LANES), f32),
                vm((n, height, LANES), f32),
                vm((n, height + extra, LANES), f32),
                vm((batch, cols), f32),
                vm((rows, cols), f32),
                vm((rows, cols), f32),
                dma((5,)), dma((half,)), dma((half,)), dma((half,)), dma((half,)),
                dma((n,)), dma((n,)), dma((n,)), dma((n,)), dma((n,)), dma((n,)), dma((n,)), dma((n,)), dma((4,)), dma((4,)),
            ],
            compiler_params=pltpu.CompilerParams(
                collective_id=0, has_side_effects=True, vmem_limit_bytes=min(56, 8 + 3 * n) * 2**20
            ),
        )(*[
            pltpu.with_memory_space_constraint(v, pltpu.HBM)
            for v in (dataset, centers, weights, batch_index, targets)
        ], gamma)
        return pl.pallas_call(
            hand_over,
            out_shape=outs,
            in_specs=[pl.BlockSpec(memory_space=pltpu.VMEM)] * 2,
            out_specs=(anywhere, anywhere),
            scratch_shapes=[dma((2,))],
            compiler_params=pltpu.CompilerParams(vmem_limit_bytes=4 * 2**20),
        )(*results)

    return jax.shard_map(
        per_device,
        mesh=mesh,
        in_specs=(
            P(("groups", "center", "row"), None),
            P(("groups", "center"), None),
            P(("groups", "center"), "row"),
            P(None, ("groups", "center", "row")),
            P(None, ("groups", "center", "row"), None),
            P("groups"),
        ),
        out_specs=(P(("groups", "center"), "row"), P(("groups", "center", "row"), None)),
        check_vma=False,
    )
```

```python
import functools

import jax
import jax.numpy as jnp
from jax import lax
from jax.experimental import pallas as pl
from jax.experimental.pallas import tpu as pltpu
from jax.sharding import PartitionSpec as P

MESH = pl.DeviceIdType.MESH
LANES = 128
NN = (((1,), (0,)), ((), ()))
NT = (((1,), (1,)), ((), ()))
UNROLL = 8


def split(v):
    hi = v.astype(jnp.bfloat16)
    return hi, (v - hi.astype(jnp.float32)).astype(jnp.bfloat16)


def dot3(a, b, dims=NN):
    (ah, al), (bh, bl) = a, b
    return lax.dot_general(
        jnp.concatenate([ah, al, ah], axis=1),
        jnp.concatenate([bh, bh, bl], axis=dims[0][1][0]),
        dims,
        preferred_element_type=jnp.float32,
    )


def each(lo, hi, body):
    if hi - lo <= UNROLL:
        for d in range(lo, hi):
            body(d)
    else:
        lax.fori_loop(lo, hi, lambda d, _: (body(d), 0)[1], 0)


def kernel(
    n, ds_hbm, cen_hbm, w_hbm, idx_hbm, tgt_hbm, gam_ref, w_out, res_out,
    ds_ref, cen_ref, w_ref, idx_ref, tgt_ref,
    xbuf, kbuf, tsib, tplace, part, rs_in, partq, rs_inq, sums, sumsq, res_s, rsend, rrecv,
    in_s, x_ss, x_rs, f_ss, f_rs, p_ss, p_rs, q_ss, q_rs, a_ss, a_rs, b_ss, b_rs, s_ss, s_rs,
):
    f32 = jnp.float32
    c, r = lax.axis_index("center"), lax.axis_index("row")
    sib = 1 - r
    half = n // 2
    h, side = c // 2, lax.rem(c, 2)
    place = side * half + h
    steps, rows = idx_ref.shape
    slot = steps * rows
    batch = 2 * rows * n
    cols = w_ref.shape[1]
    ncen = cen_ref.shape[0]
    rate = 0.5 / batch
    fold, rg, pw, gw = sizes(n, batch, cols)

    ins = [
        pltpu.make_async_copy(src, dst, in_s.at[i])
        for i, (src, dst) in enumerate(
            [(idx_hbm, idx_ref), (ds_hbm, ds_ref), (tgt_hbm, tgt_ref), (cen_hbm, cen_ref), (w_hbm, w_ref)]
        )
    ]
    for one in ins:
        one.start()

    barrier = pltpu.get_barrier_semaphore()

    def to(d):
        return {"center": lax.rem(c + d, n), "row": r}

    to_sib = {"center": c, "row": sib}
    to_pair = {"center": 2 * h + 1 - side, "row": r}
    each(1, n, lambda d: pl.semaphore_signal(barrier, inc=1, device_id=to(d), device_id_type=MESH))
    pl.semaphore_signal(barrier, inc=1, device_id=to_sib, device_id_type=MESH)

    def copy(src, dst, ss, rs, peer):
        return pltpu.make_async_remote_copy(
            src_ref=src, dst_ref=dst, send_sem=ss, recv_sem=rs, device_id=peer, device_id_type=MESH
        )

    ins[0].wait()
    ins[1].wait()
    for b in range(steps):
        for i in range(rows):
            xbuf[place, pl.ds(b * rows + i, 1), :] = ds_ref[pl.ds(idx_ref[b, i], 1), :]
    ins[2].wait()

    pl.semaphore_wait(barrier, n)

    def x_copy(e):
        peer = {"center": 2 * lax.rem(h + e, half) + side, "row": r}
        return copy(xbuf.at[place], xbuf.at[place], x_ss.at[e], x_rs.at[e], peer)

    def f_copy(e):
        at = side * half + lax.rem(h + half - e, half)
        return copy(xbuf.at[at], xbuf.at[at], f_ss.at[e], f_rs.at[e], to_pair)

    each(1, half, lambda e: x_copy(e).start())
    f_copy(0).start()
    sib_cols = pl.ds(pl.multiple_of(sib * cols, LANES), cols)
    own_cols = pl.ds(pl.multiple_of(r * cols, LANES), cols)
    t_copy = copy(tgt_ref.at[:, :, sib_cols], tsib, s_ss.at[0], s_rs.at[0], to_sib)
    t_copy.start()

    ins[3].wait()
    cen = jnp.transpose(cen_ref[...])
    cen2 = jnp.concatenate(split(cen), axis=1)
    csq = jnp.sum(cen * cen, axis=0, keepdims=True)
    ins[4].wait()
    w2 = split(w_ref[...])
    gamma = gam_ref[0]

    def pass_on(e):
        x_copy(e).wait_recv()
        f_copy(e).start()

    each(1, half, pass_on)

    count = half * slot
    step = min(count, UNROLL * slot)

    def kernel_rows(which, s):
        first = pl.multiple_of(which * count + s * step, slot)
        x = xbuf[pl.ds(which * half + s * (step // slot), step // slot)].reshape(step, xbuf.shape[2])
        xsq = jnp.sum(x * x, axis=1, keepdims=True)
        quad = jnp.dot(jnp.concatenate(split(x), axis=0), cen2, preferred_element_type=f32)
        cross = quad[:step, :ncen] + (quad[:step, ncen:] + quad[step:, :ncen] + quad[step:, ncen:])
        kbuf[pl.ds(pl.multiple_of(r * (n * slot) + first, slot), step), :] = jnp.exp(
            -gamma * (xsq + csq - 2.0 * cross)
        )

    def k_copy(i, which):
        at = pl.ds(pl.multiple_of(r * (n * slot) + which * count, slot), count)
        return copy(kbuf.at[at, :], kbuf.at[at, :], s_ss.at[i], s_rs.at[i], to_sib)

    each(0, count // step, lambda s: kernel_rows(side, s))
    k_copy(1, side).start()

    t_copy.wait()
    place_id = lax.broadcasted_iota(jnp.int32, (n, cols), 0)
    for j in range(slot):
        b, i = divmod(j, rows)
        tplace[0, j * n : (j + 1) * n, :] = jnp.where(place_id == place, tgt_ref[b, i : i + 1, own_cols], 0.0)
        tplace[1, j * n : (j + 1) * n, :] = jnp.where(place_id == place, tsib[b, i : i + 1, :], 0.0)

    each(0, half, lambda e: f_copy(e).wait_recv())
    each(0, count // step, lambda s: kernel_rows(1 - side, s))
    k_copy(2, 1 - side).start()

    def core_rows(core):
        return jnp.concatenate(
            [kbuf[pl.ds(core * (n * slot) + j, n, stride=slot), :] for j in range(slot)], axis=0
        )

    def predict(which):
        return dot3(split(kernels[which]), w2) - tplace[which]

    def put(ref, values, at, size):
        for l in range(values.shape[1] // LANES):
            for o in range(n):
                ref[o, at + l * size : at + (l + 1) * size, :] = values[
                    o * size : (o + 1) * size, l * LANES : (l + 1) * LANES
                ]

    def p_copy(d):
        return copy(part.at[lax.rem(c + d, n)], rs_in.at[d], p_ss.at[d], p_rs.at[d], to(d))

    def q_copy(d):
        return copy(partq.at[lax.rem(c + d, n)], rs_inq.at[d], q_ss.at[d], q_rs.at[d], to(d))

    kernels = [core_rows(r)]
    put(part, predict(0), 0, slot)
    each(1, n, lambda d: p_copy(d).start())

    k_copy(1, side).wait()
    k_copy(2, 1 - side).wait()
    kernels.append(core_rows(sib))
    put(partq, predict(1), 0, slot)
    k_0 = jnp.concatenate([v[: rows * n] for v in kernels], axis=0)
    k_1 = jnp.concatenate([v[rows * n :] for v in kernels], axis=0)
    k0h, k0l = split(k_0)
    k0f = (jnp.concatenate([k0h] * fold, axis=0), jnp.concatenate([k0l] * fold, axis=0))
    put(partq, fold_rows(dot3(split(k_1), k0f, NT), fold, batch), pw * slot, rg)
    each(1, n, lambda d: q_copy(d).start())

    k_t = split(jnp.transpose(jnp.concatenate([k_0, k_1], axis=0)))
    sums[c] = part[c]
    sumsq[c] = partq[c]

    def add(d):
        p_copy(d).wait_recv()
        sums[c] += rs_in[d]

    def addq(d):
        q_copy(d).wait_recv()
        sumsq[c] += rs_inq[d]

    def a_copy(d):
        return copy(sums.at[c], sums.at[c], a_ss.at[d], a_rs.at[d], to(d))

    def b_copy(d):
        return copy(sumsq.at[c], sumsq.at[c], b_ss.at[d], b_rs.at[d], to(d))

    each(1, n, add)
    each(1, n, lambda d: a_copy(d).start())
    each(1, n, addq)
    each(1, n, lambda d: b_copy(d).start())
    each(1, n, lambda d: a_copy(d).wait_recv())
    each(1, n, lambda d: b_copy(d).wait_recv())

    def take(ref, at, size, width, owners):
        pieces = [
            jnp.concatenate([ref[o, at + l * size : at + (l + 1) * size, :] for o in owners], axis=0)
            for l in range(width)
        ]
        return pieces[0] if width == 1 else jnp.concatenate(pieces, axis=1)

    def both_cores(owners):
        return jnp.concatenate([take(ref, 0, slot, pw, owners) for ref in (sums, sumsq)], axis=0)

    g = unfold_rows(take(sumsq, pw * slot, rg, gw, range(n)), fold, batch)
    res0h, res0l = split(both_cores(range(n // 2)))
    res0f = (jnp.concatenate([res0h] * fold, axis=0), jnp.concatenate([res0l] * fold, axis=0))
    res1 = both_cores(range(n // 2, n)) - rate * dot3(split(g), res0f)
    res_s[...] = res1
    for i in range(rows):
        rsend[i : i + 1, :] = res_s[pl.ds((rows + i) * n + place, 1), :]
    r_copy = copy(rsend, rrecv, s_ss.at[3], s_rs.at[3], to_sib)
    r_copy.start()
    for i in range(rows):
        res_out[i : i + 1, own_cols] = res_s[pl.ds(i * n + place, 1), :]
    res1h, res1l = split(res1)
    res = (jnp.concatenate([res0h, res1h], axis=0), jnp.concatenate([res0l, res1l], axis=0))
    w_out[...] = w_ref[...] - rate * dot3(k_t, res)
    r_copy.wait()
    res_out[:, sib_cols] = rrecv[...]

    def drain(d):
        p_copy(d).wait_send()
        q_copy(d).wait_send()
        a_copy(d).wait_send()
        b_copy(d).wait_send()

    each(1, n, drain)
    each(1, half, lambda e: x_copy(e).wait_send())
    each(0, half, lambda e: f_copy(e).wait_send())


def sizes(n, batch, cols):
    fold = max(1, LANES // batch)
    return fold, batch // fold // n, cols // LANES, pl.cdiv(batch, LANES)


def fold_rows(g, fold, batch):
    if fold == 1:
        return g
    height = g.shape[0] // fold
    at = lax.broadcasted_iota(jnp.int32, (height, LANES), 1) // batch
    out = g[:height]
    for f in range(1, fold):
        out = jnp.where(at == f, g[f * height : (f + 1) * height], out)
    return out


def unfold_rows(g, fold, batch):
    if fold == 1:
        return g
    at = lax.broadcasted_iota(jnp.int32, g.shape, 1) // batch
    return jnp.concatenate([jnp.where(at == f, g, 0.0) for f in range(fold)], axis=0)


def hand_over(w_in, res_in, w_out, res_out, sems):
    copies = [
        pltpu.make_async_copy(w_in, w_out, sems.at[0]),
        pltpu.make_async_copy(res_in, res_out, sems.at[1]),
    ]
    for one in copies:
        one.start()
    for one in copies:
        one.wait()


def solution(mesh):
    n = mesh.shape["center"]

    def per_device(dataset, centers, weights, batch_index, targets, gamma):
        f32 = jnp.float32
        steps, rows = batch_index.shape
        slot, feats = steps * rows, dataset.shape[1]
        ncen, cols = weights.shape
        total, batch = slot * 2 * n, rows * 2 * n
        fold, rg, pw, gw = sizes(n, batch, cols)
        height, extra = pw * slot, gw * rg
        half = n // 2
        vm = pltpu.VMEM
        dma = pltpu.SemaphoreType.DMA
        anywhere = pl.BlockSpec(memory_space=pltpu.HBM)
        outs = (
            jax.ShapeDtypeStruct(weights.shape, f32),
            jax.ShapeDtypeStruct(targets.shape[1:], f32),
        )
        results = pl.pallas_call(
            functools.partial(kernel, n),
            out_shape=outs,
            in_specs=[anywhere] * 5 + [pl.BlockSpec(memory_space=pltpu.SMEM)],
            out_specs=(pl.BlockSpec(memory_space=pltpu.VMEM), pl.BlockSpec(memory_space=pltpu.VMEM)),
            scratch_shapes=[
                vm(dataset.shape, f32), vm(centers.shape, f32), vm(weights.shape, f32),
                pltpu.SMEM(batch_index.shape, jnp.int32), vm(targets.shape, f32),
                vm((n, slot, feats), f32),
                vm((2 * n * slot, ncen), f32),
                vm((steps, rows, cols), f32),
                vm((2, total // 2, cols), f32),
                vm((n, height, LANES), f32),
                vm((n, height, LANES), f32),
                vm((n, height + extra, LANES), f32),
                vm((n, height + extra, LANES), f32),
                vm((n, height, LANES), f32),
                vm((n, height + extra, LANES), f32),
                vm((batch, cols), f32),
                vm((rows, cols), f32),
                vm((rows, cols), f32),
                dma((5,)), dma((half,)), dma((half,)), dma((half,)), dma((half,)),
                dma((n,)), dma((n,)), dma((n,)), dma((n,)), dma((n,)), dma((n,)), dma((n,)), dma((n,)), dma((4,)), dma((4,)),
            ],
            compiler_params=pltpu.CompilerParams(
                collective_id=0, has_side_effects=True, vmem_limit_bytes=min(56, 8 + 3 * n) * 2**20
            ),
        )(*[
            pltpu.with_memory_space_constraint(v, pltpu.HBM)
            for v in (dataset, centers, weights, batch_index, targets)
        ], gamma)
        return pl.pallas_call(
            hand_over,
            out_shape=outs,
            in_specs=[pl.BlockSpec(memory_space=pltpu.VMEM)] * 2,
            out_specs=(anywhere, anywhere),
            scratch_shapes=[dma((2,))],
            compiler_params=pltpu.CompilerParams(vmem_limit_bytes=4 * 2**20),
        )(*results)

    return jax.shard_map(
        per_device,
        mesh=mesh,
        in_specs=(
            P(("groups", "center", "row"), None),
            P(("groups", "center"), None),
            P(("groups", "center"), "row"),
            P(None, ("groups", "center", "row")),
            P(None, ("groups", "center", "row"), None),
            P("groups"),
        ),
        out_specs=(P(("groups", "center"), "row"), P(("groups", "center", "row"), None)),
        check_vma=False,
    )
```

```python
import functools

import jax
import jax.numpy as jnp
from jax import lax
from jax.experimental import pallas as pl
from jax.experimental.pallas import tpu as pltpu
from jax.sharding import PartitionSpec as P

MESH = pl.DeviceIdType.MESH
LANES = 128
NN = (((1,), (0,)), ((), ()))
NT = (((1,), (1,)), ((), ()))
UNROLL = 8


def split(v):
    hi = v.astype(jnp.bfloat16)
    return hi, (v - hi.astype(jnp.float32)).astype(jnp.bfloat16)


def dot3(a, b, dims=NN):
    (ah, al), (bh, bl) = a, b
    return lax.dot_general(
        jnp.concatenate([ah, al, ah], axis=1),
        jnp.concatenate([bh, bh, bl], axis=dims[0][1][0]),
        dims,
        preferred_element_type=jnp.float32,
    )


def each(lo, hi, body):
    if hi - lo <= UNROLL:
        for d in range(lo, hi):
            body(d)
    else:
        lax.fori_loop(lo, hi, lambda d, _: (body(d), 0)[1], 0)


def kernel(
    n, ds_hbm, cen_hbm, w_hbm, idx_hbm, tgt_hbm, gam_ref, w_out, res_out,
    ds_ref, cen_ref, w_ref, idx_ref, tgt_ref,
    xbuf, kbuf, tsib, tplace, part, rs_in, partq, rs_inq, sums, sumsq, res_s, rsend, rrecv,
    in_s, x_ss, x_rs, f_ss, f_rs, p_ss, p_rs, q_ss, q_rs, a_ss, a_rs, b_ss, b_rs, s_ss, s_rs,
):
    f32 = jnp.float32
    c, r = lax.axis_index("center"), lax.axis_index("row")
    sib = 1 - r
    half = n // 2
    h, side = c // 2, lax.rem(c, 2)
    place = side * half + h
    steps, rows = idx_ref.shape
    slot = steps * rows
    batch = 2 * rows * n
    cols = w_ref.shape[1]
    ncen = cen_ref.shape[0]
    rate = 0.5 / batch
    first, owners, fold, rp, rg, pw, gw = sizes(n, batch, cols, steps)

    ins = [
        pltpu.make_async_copy(src, dst, in_s.at[i])
        for i, (src, dst) in enumerate(
            [(idx_hbm, idx_ref), (ds_hbm, ds_ref), (tgt_hbm, tgt_ref), (cen_hbm, cen_ref), (w_hbm, w_ref)]
        )
    ]
    barrier = pltpu.get_barrier_semaphore()

    def to(d):
        return {"center": lax.rem(c + d, n), "row": r}

    to_sib = {"center": c, "row": sib}
    each(1, n, lambda d: pl.semaphore_signal(barrier, inc=1, device_id=to(d), device_id_type=MESH))
    pl.semaphore_signal(barrier, inc=1, device_id=to_sib, device_id_type=MESH)
    for one in ins:
        one.start()

    def copy(src, dst, ss, rs, peer):
        return pltpu.make_async_remote_copy(
            src_ref=src, dst_ref=dst, send_sem=ss, recv_sem=rs, device_id=peer, device_id_type=MESH
        )

    ins[0].wait()
    ins[1].wait()
    for b in range(steps):
        for i in range(rows):
            xbuf[place, pl.ds(b * rows + i, 1), :] = ds_ref[pl.ds(idx_ref[b, i], 1), :]

    pl.semaphore_wait(barrier, n)

    def x_copy(e):
        peer = {"center": 2 * lax.rem(h + e, half) + side, "row": r}
        return copy(xbuf.at[place], xbuf.at[place], x_ss.at[e], x_rs.at[e], peer)

    def f_copy(e):
        peer = {"center": 2 * lax.rem(h + e, half) + 1 - side, "row": r}
        return copy(xbuf.at[place], xbuf.at[place], f_ss.at[e], f_rs.at[e], peer)

    each(1, half, lambda e: x_copy(e).start())
    each(0, half, lambda e: f_copy(e).start())
    sib_cols = pl.ds(pl.multiple_of(sib * cols, LANES), cols)
    own_cols = pl.ds(pl.multiple_of(r * cols, LANES), cols)
    t_copy = copy(tgt_ref.at[:, :, sib_cols], tsib, s_ss.at[0], s_rs.at[0], to_sib)
    ins[2].wait()
    t_copy.start()

    ins[3].wait()
    cen = jnp.transpose(cen_ref[...])
    cen2 = jnp.concatenate(split(cen), axis=1)
    csq = jnp.sum(cen * cen, axis=0, keepdims=True)
    ins[4].wait()
    w2 = split(w_ref[...])
    gamma = gam_ref[0]

    each(1, half, lambda e: x_copy(e).wait_recv())

    count = half * slot
    step = min(count, UNROLL * slot)

    def kernel_rows(which, s):
        first = pl.multiple_of(which * count + s * step, slot)
        x = xbuf[pl.ds(which * half + s * (step // slot), step // slot)].reshape(step, xbuf.shape[2])
        xsq = jnp.sum(x * x, axis=1, keepdims=True)
        quad = jnp.dot(jnp.concatenate(split(x), axis=0), cen2, preferred_element_type=f32)
        cross = quad[:step, :ncen] + (quad[:step, ncen:] + quad[step:, :ncen] + quad[step:, ncen:])
        kbuf[pl.ds(pl.multiple_of(r * (n * slot) + first, slot), step), :] = jnp.exp(
            -gamma * (xsq + csq - 2.0 * cross)
        )

    def k_copy(i, which):
        at = pl.ds(pl.multiple_of(r * (n * slot) + which * count, slot), count)
        return copy(kbuf.at[at, :], kbuf.at[at, :], s_ss.at[i], s_rs.at[i], to_sib)

    each(0, count // step, lambda s: kernel_rows(side, s))
    k_copy(1, side).start()

    t_copy.wait()
    place_id = lax.broadcasted_iota(jnp.int32, (n, cols), 0)
    for j in range(slot):
        b, i = divmod(j, rows)
        tplace[0, j * n : (j + 1) * n, :] = jnp.where(place_id == place, tgt_ref[b, i : i + 1, own_cols], 0.0)
        tplace[1, j * n : (j + 1) * n, :] = jnp.where(place_id == place, tsib[b, i : i + 1, :], 0.0)

    each(0, half, lambda e: f_copy(e).wait_recv())
    each(0, count // step, lambda s: kernel_rows(1 - side, s))
    k_copy(2, 1 - side).start()

    def core_rows(core):
        return jnp.concatenate(
            [kbuf[pl.ds(core * (n * slot) + j, n, stride=slot), :] for j in range(slot)], axis=0
        )

    def predict(which):
        return dot3(split(kernels[which]), w2) - tplace[which]

    def put(ref, values, at, size):
        for l in range(values.shape[1] // LANES):
            for o in range(owners):
                ref[o, at + l * size : at + (l + 1) * size, :] = values[
                    o * size : (o + 1) * size, l * LANES : (l + 1) * LANES
                ]

    def owns(device):
        return jnp.logical_and(device >= first, device < first + owners)

    def p_copy(d, at):
        return copy(part.at[at], rs_in.at[d], p_ss.at[d], p_rs.at[d], to(d))

    def q_copy(d, at):
        return copy(partq.at[at], rs_inq.at[d], q_ss.at[d], q_rs.at[d], to(d))

    def to_owners(body):
        def one(d):
            at = lax.rem(c + d, n)
            pl.when(owns(at))(lambda: body(d, at - first))

        each(1, n, one)

    kernels = [core_rows(r)]
    put(part, predict(0), 0, rp)
    to_owners(lambda d, at: p_copy(d, at).start())

    k_copy(1, side).wait()
    k_copy(2, 1 - side).wait()
    kernels.append(core_rows(sib))
    put(partq, predict(1), 0, rp)
    k_0 = jnp.concatenate([v[: rows * n] for v in kernels], axis=0)
    k_1 = jnp.concatenate([v[rows * n :] for v in kernels], axis=0)
    k0h, k0l = split(k_0)
    k0f = (jnp.concatenate([k0h] * fold, axis=0), jnp.concatenate([k0l] * fold, axis=0))
    put(partq, fold_rows(dot3(split(k_1), k0f, NT), fold, batch), pw * rp, rg)
    to_owners(lambda d, at: q_copy(d, at).start())

    k_t = split(jnp.transpose(jnp.concatenate([k_0, k_1], axis=0)))

    def gathered(ref, at, ss, rs, d):
        return copy(ref.at[at - first], ref.at[at - first], ss.at[d], rs.at[d], to(d))

    def a_copy(at, d):
        return gathered(sums, at, a_ss, a_rs, d)

    def b_copy(at, d):
        return gathered(sumsq, at, b_ss, b_rs, d)

    @pl.when(owns(c))
    def _():
        me = c - first
        sums[me] = part[me]
        sumsq[me] = partq[me]

        def add(d):
            p_copy(d, me).wait_recv()
            sums[me] += rs_in[d]

        def addq(d):
            q_copy(d, me).wait_recv()
            sumsq[me] += rs_inq[d]

        each(1, n, add)
        each(1, n, lambda d: a_copy(c, d).start())
        each(1, n, addq)
        each(1, n, lambda d: b_copy(c, d).start())

    def arrive(d):
        at = lax.rem(c + n - d, n)

        @pl.when(owns(at))
        def _():
            a_copy(at, d).wait_recv()
            b_copy(at, d).wait_recv()

    each(1, n, arrive)

    def take(ref, at, size, width, which):
        pieces = [
            jnp.concatenate([ref[o, at + l * size : at + (l + 1) * size, :] for o in which], axis=0)
            for l in range(width)
        ]
        return pieces[0] if width == 1 else jnp.concatenate(pieces, axis=1)

    def both_cores(which):
        return jnp.concatenate([take(ref, 0, rp, pw, which) for ref in (sums, sumsq)], axis=0)

    g = unfold_rows(take(sumsq, pw * rp, rg, gw, range(owners)), fold, batch)
    res0h, res0l = split(both_cores(range(owners // 2)))
    res0f = (jnp.concatenate([res0h] * fold, axis=0), jnp.concatenate([res0l] * fold, axis=0))
    res1 = both_cores(range(owners // 2, owners)) - rate * dot3(split(g), res0f)
    res_s[...] = res1
    for i in range(rows):
        rsend[i : i + 1, :] = res_s[pl.ds((rows + i) * n + place, 1), :]
    r_copy = copy(rsend, rrecv, s_ss.at[3], s_rs.at[3], to_sib)
    r_copy.start()
    for i in range(rows):
        res_out[i : i + 1, own_cols] = res_s[pl.ds(i * n + place, 1), :]
    res1h, res1l = split(res1)
    res = (jnp.concatenate([res0h, res1h], axis=0), jnp.concatenate([res0l, res1l], axis=0))
    w_out[...] = w_ref[...] - rate * dot3(k_t, res)
    r_copy.wait()
    res_out[:, sib_cols] = rrecv[...]

    to_owners(lambda d, at: (p_copy(d, at).wait_send(), q_copy(d, at).wait_send())[0])

    @pl.when(owns(c))
    def _():
        each(1, n, lambda d: a_copy(c, d).wait_send())
        each(1, n, lambda d: b_copy(c, d).wait_send())

    each(1, half, lambda e: x_copy(e).wait_send())
    each(0, half, lambda e: f_copy(e).wait_send())


def sizes(n, batch, cols, steps):
    first = n // 4 if n % 8 == 0 else 0
    owners = n - 2 * first
    fold = max(1, LANES // batch)
    return first, owners, fold, steps * batch // 2 // owners, batch // fold // owners, cols // LANES, pl.cdiv(batch, LANES)


def fold_rows(g, fold, batch):
    if fold == 1:
        return g
    height = g.shape[0] // fold
    at = lax.broadcasted_iota(jnp.int32, (height, LANES), 1) // batch
    out = g[:height]
    for f in range(1, fold):
        out = jnp.where(at == f, g[f * height : (f + 1) * height], out)
    return out


def unfold_rows(g, fold, batch):
    if fold == 1:
        return g
    at = lax.broadcasted_iota(jnp.int32, g.shape, 1) // batch
    return jnp.concatenate([jnp.where(at == f, g, 0.0) for f in range(fold)], axis=0)


def hand_over(w_in, res_in, w_out, res_out, sems):
    copies = [
        pltpu.make_async_copy(w_in, w_out, sems.at[0]),
        pltpu.make_async_copy(res_in, res_out, sems.at[1]),
    ]
    for one in copies:
        one.start()
    for one in copies:
        one.wait()


def solution(mesh):
    n = mesh.shape["center"]

    def per_device(dataset, centers, weights, batch_index, targets, gamma):
        f32 = jnp.float32
        steps, rows = batch_index.shape
        slot, feats = steps * rows, dataset.shape[1]
        ncen, cols = weights.shape
        total, batch = slot * 2 * n, rows * 2 * n
        _, owners, fold, rp, rg, pw, gw = sizes(n, batch, cols, steps)
        height, extra = pw * rp, gw * rg
        half = n // 2
        vm = pltpu.VMEM
        dma = pltpu.SemaphoreType.DMA
        anywhere = pl.BlockSpec(memory_space=pltpu.HBM)
        outs = (
            jax.ShapeDtypeStruct(weights.shape, f32),
            jax.ShapeDtypeStruct(targets.shape[1:], f32),
        )
        results = pl.pallas_call(
            functools.partial(kernel, n),
            out_shape=outs,
            in_specs=[anywhere] * 5 + [pl.BlockSpec(memory_space=pltpu.SMEM)],
            out_specs=(pl.BlockSpec(memory_space=pltpu.VMEM), pl.BlockSpec(memory_space=pltpu.VMEM)),
            scratch_shapes=[
                vm(dataset.shape, f32), vm(centers.shape, f32), vm(weights.shape, f32),
                pltpu.SMEM(batch_index.shape, jnp.int32), vm(targets.shape, f32),
                vm((n, slot, feats), f32),
                vm((2 * n * slot, ncen), f32),
                vm((steps, rows, cols), f32),
                vm((2, total // 2, cols), f32),
                vm((owners, height, LANES), f32),
                vm((n, height, LANES), f32),
                vm((owners, height + extra, LANES), f32),
                vm((n, height + extra, LANES), f32),
                vm((owners, height, LANES), f32),
                vm((owners, height + extra, LANES), f32),
                vm((batch, cols), f32),
                vm((rows, cols), f32),
                vm((rows, cols), f32),
                dma((5,)), dma((half,)), dma((half,)), dma((half,)), dma((half,)),
                dma((n,)), dma((n,)), dma((n,)), dma((n,)), dma((n,)), dma((n,)), dma((n,)), dma((n,)), dma((4,)), dma((4,)),
            ],
            compiler_params=pltpu.CompilerParams(
                collective_id=0, has_side_effects=True, vmem_limit_bytes=min(56, 8 + 3 * n) * 2**20
            ),
        )(*[
            pltpu.with_memory_space_constraint(v, pltpu.HBM)
            for v in (dataset, centers, weights, batch_index, targets)
        ], gamma)
        return pl.pallas_call(
            hand_over,
            out_shape=outs,
            in_specs=[pl.BlockSpec(memory_space=pltpu.VMEM)] * 2,
            out_specs=(anywhere, anywhere),
            scratch_shapes=[dma((2,))],
            compiler_params=pltpu.CompilerParams(vmem_limit_bytes=4 * 2**20),
        )(*results)

    return jax.shard_map(
        per_device,
        mesh=mesh,
        in_specs=(
            P(("groups", "center", "row"), None),
            P(("groups", "center"), None),
            P(("groups", "center"), "row"),
            P(None, ("groups", "center", "row")),
            P(None, ("groups", "center", "row"), None),
            P("groups"),
        ),
        out_specs=(P(("groups", "center"), "row"), P(("groups", "center", "row"), None)),
        check_vma=False,
    )
```
